512 devices in a mesh: aux: 128 (over z, y, core), row: 4 (over x).
Axes of the slice: x: 4, y: 4, z: 16, core: 2. Of those that a mesh axis runs over, the one named last changes fastest.
Arguments:
- rho_real: float32 [2048, 128, 128], P('aux', 'row'), may hold values from -6 to 6
- rho_imag: float32 [2048, 128, 128], P('aux', 'row'), may hold values from -6 to 6
- hamiltonian: float32 [128, 128], replicated, may hold values from -0.5 to 0.5
- damping: float32 [2048], P('aux'), may hold values from 0.2 to 2
- couplings: int32 [2048, 3, 6], P('aux'), may hold values from 0 to 2047, as said below
- mode_vector: float32 [128, 128], replicated, may hold values from -4 to 4
- mode_coef: float32 [2, 128], replicated, may hold values from -1 to 1
Outputs:
- next_real: float32 [2048, 128, 128], P('aux', 'row')
- next_imag: float32 [2048, 128, 128], P('aux', 'row')
The draws below stay inside these ranges and needn't reach their ends.
Inputs may be any that keep to these rules, and one draw needn't show every extreme that they name: couplings[s,0,:] are target matrices below 2048, couplings[s,1,:] modes below 128, couplings[s,2,:] weights 0 to 4. The couplings of the sources held by one index of aux name targets held by any one index of aux at most 1 times, and some pair reaches 1.
All inputs are finite; a program needn't handle non-finite values.
Results may differ from the reference program's by a relative error of at most 0.0018.
Values may be sent and summed in bfloat16 or wider, within the bound.
No kernel may reach another device: no remote copies, remote signals or barrier semaphores. Data moves between devices by JAX's collectives and lax.ppermute only.
A program may use at most 64 MiB of HBM per device.

```python
import math
import jax
import jax.numpy as jnp
from jax import lax

PIG = 128
MODES = 128
LINKS = 6
STEPS = 1
AUX_DEV = 16
AUX = 2048
N_AUX = 128


def draw_couplings(key, part):
    key = jax.random.fold_in(key, 11)
    count = AUX_DEV * LINKS
    slots = max(1, (count + N_AUX - 1) // N_AUX)
    key_perm, key_local, key_mode, key_weight = jax.random.split(key, 4)
    base = (jnp.arange(N_AUX * slots) // slots).astype(jnp.int32)
    shuffled = jax.vmap(lambda sub: jax.random.permutation(sub, base))(jax.random.split(key_perm, N_AUX))
    first_row = shuffled[0]
    where_last = jnp.argmax((first_row == N_AUX - 1).astype(jnp.int32)).astype(jnp.int32)
    first_row = jnp.roll(first_row, -where_last)
    shuffled = shuffled.at[0].set(first_row)
    dest = shuffled[:, :count]
    local = jax.random.randint(key_local, (N_AUX, count), 0, AUX_DEV)
    local = local.at[0, 0].set(AUX_DEV - 1)
    target = dest * AUX_DEV + local
    modes = jax.random.randint(key_mode, (N_AUX, count), 0, MODES)
    modes = modes.at[0, 0].set(MODES - 1)
    weight = jax.random.randint(key_weight, (N_AUX, count), 0, 5)
    weight = weight.at[0, 0].set(0)
    stacked = jnp.stack([target.reshape(AUX, LINKS), modes.reshape(AUX, LINKS), weight.reshape(AUX, LINKS)], axis=1)
    return stacked.astype(jnp.int32)


def shard_levels(own_key, dims, cuts, low, top_value):
    level = 1.0
    for axis_at, shards_of in cuts:
        draws = jax.random.uniform(jax.random.fold_in(jax.random.fold_in(own_key, 6), axis_at), (shards_of,), jnp.float32, low / len(cuts), top_value / len(cuts))
        level = level * jnp.repeat(jnp.exp(draws), dims[axis_at] // shards_of).reshape((-1,) + (1,) * (len(dims) - 1 - axis_at))
    return level


def centred(rng, dims, width, reach, pieces=(), dtype=jnp.bfloat16):
    entries = width * jax.random.normal(rng, dims, jnp.float32)
    if pieces:
        entries = entries * shard_levels(rng, dims, pieces, -0.22, 0.18)
    return jnp.clip(entries, -reach, reach).astype(dtype)


def setup_inputs(seed: int = 0) -> dict:
    keys = jax.random.split(jax.random.key(seed), 8)
    return {
        "rho_real": centred(keys[0], (AUX, PIG, PIG), 1.0, 6.0, ((0, 128), (1, 4)), jnp.float32),
        "rho_imag": centred(keys[1], (AUX, PIG, PIG), 1.0, 6.0, ((0, 128), (1, 4)), jnp.float32),
        "hamiltonian": centred(keys[2], (PIG, PIG), PIG ** -0.5, 0.5, (), jnp.float32),
        "damping": jnp.clip(jnp.exp(math.log(2.0) - 2.3025851 * jax.random.uniform(keys[3], (AUX,), jnp.float32) ** shard_levels(keys[3], (AUX,), ((0, 128),), -0.2, 0.2)), 0.2, 2.0),
        "couplings": draw_couplings(jax.random.fold_in(keys[7], 71), 0),
        "mode_vector": centred(keys[5], (MODES, PIG), 1.5, 4.0, (), jnp.float32),
        "mode_coef": jnp.clip(jax.random.uniform(keys[6], (2, MODES), jnp.float32, -1.0, 1.0), -1.0, 1.0),
    }


step_size = 0.1
high = lax.Precision.HIGHEST


def rounded(values):
    return lax.optimization_barrier(values.astype(jnp.bfloat16)).astype(jnp.float32)


def derivative(real_part, imag_part, energy, damping, couplings, mode_vector, mode_coef):
    prod_real = jnp.einsum("ij,ajk->aik", energy, real_part, precision=high) - jnp.einsum("aij,jk->aik", real_part, energy, precision=high)
    prod_imag = jnp.einsum("ij,ajk->aik", energy, imag_part, precision=high) - jnp.einsum("aij,jk->aik", imag_part, energy, precision=high)
    rate = damping[:, None, None]
    out_real = prod_imag - rate * real_part
    out_imag = -prod_real - rate * imag_part
    for column in range(LINKS):
        target = couplings[:, 0, column].astype(jnp.int32)
        modes = couplings[:, 1, column]
        weight = couplings[:, 2, column]
        vectors = mode_vector[modes]
        scaled = weight.astype(jnp.float32)
        plus = scaled * mode_coef[1][modes]
        minus = jnp.where(weight == 0, 1.0, scaled * mode_coef[0][modes])
        summed = vectors[:, :, None] + vectors[:, None, :]
        differ = vectors[:, :, None] - vectors[:, None, :]
        fac_real = plus[:, None, None] * summed
        fac_imag = -(minus[:, None, None] * differ)
        term_real = rounded(fac_real * real_part - fac_imag * imag_part)
        term_imag = rounded(fac_real * imag_part + fac_imag * real_part)
        out_real = out_real.at[target].add(term_real)
        out_imag = out_imag.at[target].add(term_imag)
    return out_real, out_imag


def reference(rho_real, rho_imag, hamiltonian, damping, couplings, mode_vector, mode_coef):
    energy = 0.5 * (hamiltonian + hamiltonian.T)

    def slope(real_part, imag_part):
        return derivative(real_part, imag_part, energy, damping, couplings, mode_vector, mode_coef)

    state_real, state_imag = rho_real, rho_imag
    for step in range(STEPS):
        one_real, one_imag = slope(state_real, state_imag)
        two_real, two_imag = slope(state_real + 0.5 * step_size * one_real, state_imag + 0.5 * step_size * one_imag)
        three_real, three_imag = slope(state_real + 0.5 * step_size * two_real, state_imag + 0.5 * step_size * two_imag)
        four_real, four_imag = slope(state_real + step_size * three_real, state_imag + step_size * three_imag)
        state_real = state_real + (step_size / 6.0) * (one_real + 2.0 * two_real + 2.0 * three_real + four_real)
        state_imag = state_imag + (step_size / 6.0) * (one_imag + 2.0 * two_imag + 2.0 * three_imag + four_imag)
    return state_real, state_imag
```

```python
import functools

import jax
import jax.numpy as jnp
from jax import lax
from jax.experimental import pallas as pl
from jax.experimental.pallas import tpu as pltpu
from jax.sharding import PartitionSpec as P

step_size = 0.1
weights_of = (step_size, step_size**2 / 2.0, step_size**3 / 6.0, step_size**4 / 24.0)
repay = weights_of[0] / weights_of[1]
high = lax.Precision.HIGHEST
f32 = jnp.float32
bf16 = jnp.bfloat16


def swap_blocks(parts):
    chunk = lax.broadcasted_iota(jnp.int32, (32, 128), 1) // 32
    rows = []
    for j in range(4):
        row = None
        for i in range(4):
            shift = (32 * (i - j)) % 128
            moved = parts[i] if shift == 0 else pltpu.roll(parts[i], shift, 1)
            row = moved if row is None else jnp.where(chunk == i, moved, row)
        rows.append(row)
    return rows


def split_rows(block):
    return [block[32 * j : 32 * j + 32] for j in range(4)]


def commutator(state, energy, rate_ref):
    result = []
    for n in range(4):
        com = []
        for part in range(2):
            x = state[2 * n + part]
            left = jnp.dot(energy, x, precision=high, preferred_element_type=f32)
            right = jnp.dot(x, energy, precision=high, preferred_element_type=f32)
            com.append(left - right)
        rate = rate_ref[n]
        result.append(com[1] - rate * state[2 * n])
        result.append(-com[0] - rate * state[2 * n + 1])
    return result


def load_matrices(rows_ref, first, per_dev, per_row):
    state = [[None] * 4 for _ in range(8)]
    for r in range(4):
        for k in range(2):
            block = rows_ref[pl.ds(per_row * r + first + k, 128, stride=per_dev), :]
            swapped = swap_blocks(split_rows(block))
            for c in range(4):
                state[4 * k + c][r] = swapped[c]
    return [jnp.concatenate(parts, axis=0) for parts in state]


def store_matrices(rows_ref, mats, first, per_dev, per_row):
    for r in range(4):
        for k in range(2):
            parts = [mats[4 * k + c][32 * r : 32 * r + 32, :] for c in range(4)]
            block = jnp.concatenate(swap_blocks(parts), axis=0)
            rows_ref[pl.ds(per_row * r + first + k, 128, stride=per_dev), :] = block


def choose(values, bits):
    for bit in bits:
        values = [jnp.where(bit, values[2 * i + 1], values[2 * i]) for i in range(len(values) // 2)]
    return values[0]


def couple(z_ref, w_ref, fac_ref, index_ref, code_ref, out_ref, exact):
    iota = lax.broadcasted_iota(jnp.int32, (128, 128), 0)

    def group(g, carry):
        index = index_ref[pl.ds(pl.multiple_of(8 * g, 8), 8), :]
        code = code_ref[pl.ds(pl.multiple_of(8 * g, 8), 8), :]
        for e in range(4):
            at_re, at_im = pl.ds(8 * e, 8), pl.ds(32 + 8 * e, 8)
            z_re = [z_ref[i, at_re, :] for i in range(16)]
            z_im = [z_ref[i, at_im, :] for i in range(16)]
            for q in range(8):
                row = jnp.broadcast_to(index[q : q + 1, :], (8, 128))
                bits = [(row & (1 << b)) != 0 for b in range(4)]
                x_re, x_im = choose(z_re, bits), choose(z_im, bits)
                fac_re, fac_im = fac_ref[8 * g + q, at_re, :], fac_ref[8 * g + q, at_im, :]
                w_ref[at_re, 128 * q : 128 * q + 128] = fac_re * x_re - fac_im * x_im
                w_ref[at_im, 128 * q : 128 * q + 128] = fac_re * x_im + fac_im * x_re
        term = w_ref[...]
        upper = term.astype(bf16)
        marks = jnp.concatenate(
            [jnp.where(iota == code[q : q + 1, :], 1.0, 0.0).astype(bf16) for q in range(8)], axis=1
        )
        dims = (((1,), (1,)), ((), ()))
        total = lax.dot_general(marks, upper, dims, preferred_element_type=f32)
        if exact:
            lower = (term - upper.astype(f32)).astype(bf16)
            total = total + lax.dot_general(marks, lower, dims, preferred_element_type=f32)
        out_ref[pl.ds(pl.multiple_of(64 * g, 64), 64), :] = jnp.concatenate([total[:64], total[64:]], axis=1)
        return carry

    lax.fori_loop(0, 16, group, 0)


def load_elements(z_ref, rows_of):
    for r in range(4):
        for k in range(2):
            turned = rows_of(r, k).T
            z_ref[4 * r + 2 * k] = turned[:64]
            z_ref[4 * r + 2 * k + 1] = turned[64:]


def pack_kernel(re_ref, im_ref, send_ref, cross_ref, rows_ref):
    for k in range(8):
        parts = [(re_ref, im_ref)[c % 2][2 * k + c // 2] for c in range(4)]
        rows_ref[pl.ds(k, 128, stride=8), :] = jnp.concatenate(swap_blocks(parts), axis=0)
        for c in range(4):
            cross_ref[k // 2, 4 * (k % 2) + c] = parts[c]
    send_ref[...] = rows_ref[...].astype(bf16)


def factor_kernel(table_ref, vector_ref, coef_ref, fac_ref, index_ref, code_ref, mode_ref, weight_ref):
    table = table_ref[...].astype(f32)
    index_ref[...] = table[:, 0:128].T.astype(jnp.int32)
    mode_ref[...] = table[:, 128:256].T.astype(jnp.int32)
    weight_ref[...] = table[:, 256:384].T
    code_ref[...] = table[:, 384:512].T.astype(jnp.int32) - 1

    def target(p, carry):
        mode = jnp.broadcast_to(mode_ref[pl.ds(p, 1), :], (8, 128))
        weight = weight_ref[pl.ds(p, 1), :]
        picked = jnp.take_along_axis(coef_ref[...], mode, axis=1)
        own, real, imag = picked[0:1, :], picked[1:2, :], picked[2:3, :]
        plus = weight * imag
        minus = jnp.where(weight == 0.0, 1.0, weight * real)
        for e in range(4):
            other = jnp.take_along_axis(vector_ref[8 * e : 8 * e + 8, :], mode, axis=1)
            fac_ref[p, 8 * e : 8 * e + 8, :] = plus * (own + other)
            fac_ref[p, 32 + 8 * e : 40 + 8 * e, :] = -(minus * (own - other))
        return carry

    lax.fori_loop(0, 128, target, 0)


def first_kernel(
    recv_ref, cross_ref, energy_ref, rate_ref, fac_ref, index_ref, code_ref,
    send_ref, com_ref, total_ref, kept_ref, owed_ref,
    z_ref, w_ref, rows_ref,
):
    state = [jnp.concatenate([cross_ref[r, m] for r in range(4)], axis=0) for m in range(8)]
    result = commutator(state, energy_ref[...], rate_ref)
    for m in range(8):
        com_ref[m] = result[m]
        result[m] = result[m] + repay * (state[m] - state[m].astype(bf16).astype(f32))
    store_matrices(rows_ref, result, 0, 16, 4)
    total_ref[...] = jnp.zeros_like(total_ref)
    kept_ref[...] = recv_ref[...].astype(f32)
    load_elements(z_ref, lambda r, k: kept_ref[pl.ds(2 * r + k, 128, stride=8), :])
    couple(z_ref, w_ref, fac_ref, index_ref, code_ref, kept_ref, True)
    owed_ref[...] = weights_of[0] * rounded_off(kept_ref[...])
    send_elements(rows_ref, kept_ref)
    send_ref[...] = rows_ref[...].astype(bf16)


def rounded_off(x):
    return x - x.astype(bf16).astype(f32)


def send_elements(rows_ref, kept_ref):
    for k in range(8):
        rows_ref[pl.ds(4 * (k // 2) + 2 + k % 2, 128, stride=16), :] = kept_ref[pl.ds(k, 128, stride=8), :]


def next_kernel(
    j, recv_ref, com_ref, total_ref, kept_ref, owed_ref, energy_ref, rate_ref, fac_ref, index_ref, code_ref,
    send_ref, com_out, total_out, kept_out, owed_out,
    z_ref, w_ref, rows_ref,
):
    rows_ref[...] = recv_ref[...].astype(f32)
    state = load_matrices(rows_ref, 2, 16, 4)
    state = [state[m] + com_ref[m] for m in range(8)]
    result = commutator(state, energy_ref[...], rate_ref)
    for m in range(8):
        total_out[m] = total_ref[m] + weights_of[j - 1] * state[m]
        com_out[m] = result[m]
    load_elements(
        z_ref,
        lambda r, k: rows_ref[pl.ds(4 * r + k, 128, stride=16), :] + kept_ref[pl.ds(2 * r + k, 128, stride=8), :],
    )
    store_matrices(rows_ref, result, 0, 16, 4)
    couple(z_ref, w_ref, fac_ref, index_ref, code_ref, kept_out, j < 2)
    owed_out[...] = owed_ref[...] + weights_of[j] * rounded_off(kept_out[...])
    send_elements(rows_ref, kept_out)
    send_ref[...] = rows_ref[...].astype(bf16)


def last_kernel(
    recv_ref, com_ref, total_ref, kept_ref, owed_ref, energy_ref, rate_ref, fac_ref, index_ref, code_ref,
    send_ref, cross_ref,
    z_ref, w_ref, rows_ref, out_ref,
):
    rows_ref[...] = recv_ref[...].astype(f32)
    state = load_matrices(rows_ref, 2, 16, 4)
    state = [state[m] + com_ref[m] for m in range(8)]
    result = commutator(state, energy_ref[...], rate_ref)
    for m in range(8):
        total = total_ref[m] + weights_of[2] * state[m] + weights_of[3] * result[m]
        for r in range(4):
            cross_ref[r, m] = total[32 * r : 32 * r + 32, :]
    load_elements(
        z_ref,
        lambda r, k: rows_ref[pl.ds(4 * r + k, 128, stride=16), :] + kept_ref[pl.ds(2 * r + k, 128, stride=8), :],
    )
    couple(z_ref, w_ref, fac_ref, index_ref, code_ref, out_ref, False)
    send_ref[...] = (weights_of[3] * out_ref[...] + owed_ref[...]).astype(bf16)


def sum_kernel(re_ref, im_ref, recv_ref, cross_ref, re_out, im_out, rows_ref):
    rows_ref[...] = recv_ref[...].astype(f32)
    for k in range(8):
        parts = swap_blocks(split_rows(rows_ref[pl.ds(k, 128, stride=8), :]))
        for c in range(4):
            n = 2 * k + c // 2
            source, result = ((re_ref, re_out), (im_ref, im_out))[c % 2]
            result[n] = source[n] + (parts[c] + cross_ref[k // 2, 4 * (k % 2) + c])


def vmem():
    return pl.BlockSpec(memory_space=pltpu.VMEM)


def smem():
    return pl.BlockSpec(memory_space=pltpu.SMEM)


def call(kernel, ins, outs, scratch, smem_at=()):
    return pl.pallas_call(
        kernel,
        out_shape=[jax.ShapeDtypeStruct(shape, dtype) for shape, dtype in outs],
        in_specs=[smem() if i in smem_at else vmem() for i in range(len(ins))],
        out_specs=[vmem() for _ in outs],
        scratch_shapes=[pltpu.VMEM(shape, dtype) for shape, dtype in scratch],
        compiler_params=pltpu.CompilerParams(vmem_limit_bytes=40 * 1024 * 1024),
    )(*ins)


work = (((16, 64, 128), f32), ((64, 1024), f32), ((2048, 128), f32))
matrices = ((8, 128, 128), f32)
messages = ((1024, 128), f32)


def couplings_table(couplings):
    count = 96
    target = couplings[:, 0, :].reshape(count)
    dest, local = target // 16, target % 16
    code = 64 * (local % 2) + 8 * (dest % 8) + local // 2 + 1
    fields = jnp.stack(
        [jnp.arange(count, dtype=jnp.int32) // 6, couplings[:, 1, :].reshape(count), couplings[:, 2, :].reshape(count), code]
    )
    picker = (dest[:, None] == jnp.arange(128)[None, :]).astype(bf16)
    return jnp.dot(fields.astype(bf16), picker, preferred_element_type=f32).astype(bf16).reshape(1, 512)


def shards(rho_real, rho_imag, hamiltonian, damping, couplings, mode_vector, mode_coef):
    d, r = lax.axis_index("aux"), lax.axis_index("row")
    send, cross = call(
        pack_kernel, (rho_real, rho_imag), (((1024, 128), bf16), ((4, 8, 32, 128), f32)), (messages,)
    )
    table = lax.all_gather(couplings_table(couplings), "aux", axis=0, tiled=True)
    cross = lax.all_to_all(cross.reshape(4, 256, 128), "row", 0, 0, tiled=True).reshape(4, 8, 32, 128)
    recv = lax.all_to_all(send.reshape(128, 8, 128), "aux", 0, 0, tiled=True).reshape(1024, 128)

    energy = 0.5 * (hamiltonian + hamiltonian.T)
    rate = lax.dynamic_slice_in_dim(damping, 4 * r, 4)
    turned = mode_vector.T
    others = lax.dynamic_slice_in_dim(turned, 32 * (d // 32), 32, 0)
    own = lax.dynamic_slice_in_dim(turned, 32 * r + d % 32, 1, 0)
    coefs = jnp.concatenate([own, mode_coef, jnp.zeros((5, 128), f32)], axis=0)
    fac, index, code = call(
        factor_kernel,
        (table, others, coefs),
        (((128, 64, 128), f32), ((128, 128), jnp.int32), ((128, 128), jnp.int32)),
        (((128, 128), jnp.int32), ((128, 128), f32)),
    )
    fixed = (energy, rate, fac, index, code)
    held = (((2048, 128), bf16), matrices, matrices, messages, messages)
    send, com, total, kept, owed = call(first_kernel, (recv, cross) + fixed, held, work, (3,))

    def exchange(x):
        return lax.all_to_all(x.reshape(512, 4, 128), ("aux", "row"), 0, 0, tiled=True).reshape(2048, 128)

    for j in range(1, 3):
        send, com, total, kept, owed = call(
            functools.partial(next_kernel, j), (exchange(send), com, total, kept, owed) + fixed, held, work, (6,)
        )
    send, cross = call(
        last_kernel,
        (exchange(send), com, total, kept, owed) + fixed,
        (((1024, 128), bf16), ((4, 8, 32, 128), f32)),
        work + (messages,),
        (6,),
    )
    cross = lax.all_to_all(cross.reshape(4, 256, 128), "row", 0, 0, tiled=True).reshape(4, 8, 32, 128)
    recv = lax.all_to_all(send.reshape(128, 8, 128), "aux", 0, 0, tiled=True).reshape(1024, 128)
    return tuple(
        call(
            sum_kernel,
            (rho_real, rho_imag, recv, cross),
            (((16, 32, 128), f32), ((16, 32, 128), f32)),
            (messages,),
        )
    )


def solution(mesh):
    placed = (
        P("aux", "row", None),
        P("aux", "row", None),
        P(),
        P("aux"),
        P("aux", None, None),
        P(),
        P(),
    )
    return jax.shard_map(
        shards,
        mesh=mesh,
        in_specs=placed,
        out_specs=(P("aux", "row", None), P("aux", "row", None)),
        check_vma=False,
    )
```

```python
import functools

import jax
import jax.numpy as jnp
from jax import lax
from jax.experimental import pallas as pl
from jax.experimental.pallas import tpu as pltpu
from jax.sharding import PartitionSpec as P

step_size = 0.1
weights_of = (step_size, step_size**2 / 2.0, step_size**3 / 6.0, step_size**4 / 24.0)
repay = weights_of[0] / weights_of[1]
high = lax.Precision.HIGHEST
f32 = jnp.float32
bf16 = jnp.bfloat16


def swap_blocks(parts):
    chunk = lax.broadcasted_iota(jnp.int32, (32, 128), 1) // 32
    rows = []
    for j in range(4):
        row = None
        for i in range(4):
            shift = (32 * (i - j)) % 128
            moved = parts[i] if shift == 0 else pltpu.roll(parts[i], shift, 1)
            row = moved if row is None else jnp.where(chunk == i, moved, row)
        rows.append(row)
    return rows


def split_rows(block):
    return [block[32 * j : 32 * j + 32] for j in range(4)]


def commutator(state, energy, rate_ref):
    row = lax.axis_index("row")
    energy = 0.5 * (energy + energy.T)
    result = []
    for n in range(4):
        com = []
        for part in range(2):
            x = state[2 * n + part]
            left = jnp.dot(energy, x, precision=high, preferred_element_type=f32)
            right = jnp.dot(x, energy, precision=high, preferred_element_type=f32)
            com.append(left - right)
        rate = rate_ref[4 * row + n]
        result.append(com[1] - rate * state[2 * n])
        result.append(-com[0] - rate * state[2 * n + 1])
    return result


def load_matrices(rows_ref, first, per_dev, per_row):
    state = [[None] * 4 for _ in range(8)]
    for r in range(4):
        for k in range(2):
            block = rows_ref[pl.ds(per_row * r + first + k, 128, stride=per_dev), :]
            swapped = swap_blocks(split_rows(block))
            for c in range(4):
                state[4 * k + c][r] = swapped[c]
    return [jnp.concatenate(parts, axis=0) for parts in state]


def store_matrices(rows_ref, mats, first, per_dev, per_row):
    for r in range(4):
        for k in range(2):
            parts = [mats[4 * k + c][32 * r : 32 * r + 32, :] for c in range(4)]
            block = jnp.concatenate(swap_blocks(parts), axis=0)
            rows_ref[pl.ds(per_row * r + first + k, 128, stride=per_dev), :] = block


def swap_chunks(parts):
    lane = lax.broadcasted_iota(jnp.int32, (8, 128), 1)
    for s in (1, 2, 4, 8):
        odd = (lane & (8 * s)) != 0
        new = list(parts)
        for i in range(16):
            if not i & s:
                one, two = parts[i], parts[i + s]
                new[i] = jnp.where(odd, pltpu.roll(two, 8 * s, 1), one)
                new[i + s] = jnp.where(odd, two, pltpu.roll(one, 128 - 8 * s, 1))
        parts = new
    return parts


def swap_rows(x):
    lane = lax.broadcasted_iota(jnp.int32, (128, 128), 1)
    row = lax.broadcasted_iota(jnp.int32, (128, 128), 0)
    for s in (1, 2, 4, 8):
        right, low = (lane & (8 * s)) != 0, (row & s) != 0
        ahead = pltpu.roll(pltpu.roll(x, 8 * s, 1), 128 - s, 0)
        behind = pltpu.roll(pltpu.roll(x, 128 - 8 * s, 1), s, 0)
        x = jnp.where(right, jnp.where(low, x, ahead), jnp.where(low, behind, x))
    return x


def load_elements(x_ref, z_ref, rows_of):
    for r in range(4):
        for k in range(2):
            turned = rows_of(r, k).T
            z_ref[4 * r + 2 * k] = turned[:64]
            z_ref[4 * r + 2 * k + 1] = turned[64:]
    for e in range(8):
        at = pl.ds(8 * e, 8)
        for w, part in enumerate(swap_chunks([z_ref[i, at, :] for i in range(16)])):
            x_ref[w, at, :] = part


def couple(x_ref, w_ref, fac_ref, index_ref, code_ref, out_ref, exact):
    target = lax.broadcasted_iota(jnp.int32, (256, 128), 0).astype(f32).astype(bf16)
    for g in range(8):
        index = index_ref[16 * g : 16 * g + 16, :]
        code = code_ref[16 * g : 16 * g + 16, :].astype(f32).astype(bf16)
        for w in range(16):
            row = jnp.broadcast_to(index[w : w + 1, :], (8, 128))
            lanes = pl.ds(128 * w, 128)
            for e in range(4):
                at_re, at_im = pl.ds(8 * e, 8), pl.ds(32 + 8 * e, 8)
                x_re = jnp.take_along_axis(x_ref[w, at_re, :], row, axis=1)
                x_im = jnp.take_along_axis(x_ref[w, at_im, :], row, axis=1)
                fac_re, fac_im = fac_ref[16 * g + w, at_re, :], fac_ref[16 * g + w, at_im, :]
                w_ref[g, at_re, lanes] = fac_re * x_re - fac_im * x_im
                w_ref[g, at_im, lanes] = fac_re * x_im + fac_im * x_re
        term = w_ref[g]
        upper = term.astype(bf16)
        marks = jnp.concatenate(
            [jnp.where(target == code[w : w + 1, :], bf16(1), bf16(0)) for w in range(16)], axis=1
        )
        dims = (((1,), (1,)), ((), ()))
        total = lax.dot_general(marks, upper, dims, preferred_element_type=f32)
        if exact:
            lower = (term - upper.astype(f32)).astype(bf16)
            total = total + lax.dot_general(marks, lower, dims, preferred_element_type=f32)
        out_ref[128 * g : 128 * g + 128, :] = jnp.concatenate([total[:128], total[128:]], axis=1)


def rounded_off(x):
    return x - x.astype(bf16).astype(f32)


def pack_kernel(re_ref, im_ref, couplings_ref, send_ref, rows_ref):
    for k in range(8):
        parts = [(re_ref, im_ref)[c % 2][2 * k + c // 2] for c in range(4)]
        rows_ref[pl.ds(k, 128, stride=12), :] = jnp.concatenate(swap_blocks(parts), axis=0)
    lane = lax.broadcasted_iota(jnp.int32, (16, 128), 1)
    source = lax.broadcasted_iota(jnp.int32, (16, 128), 0)
    target, mode, weight = (couplings_ref[:, f, :] for f in range(3))
    fields = [jnp.zeros((16, 128), jnp.int32) for _ in range(4)]
    for j in range(6):
        to = jnp.broadcast_to(target[:, j : j + 1], (16, 128))
        here = (to // 16) == lane
        values = (
            source,
            jnp.broadcast_to(mode[:, j : j + 1], (16, 128)),
            jnp.broadcast_to(weight[:, j : j + 1], (16, 128)),
            to % 16 + 1,
        )
        fields = [field + jnp.where(here, value, 0) for field, value in zip(fields, values)]
    for f in range(4):
        line = jnp.sum(fields[f].astype(f32), axis=0, keepdims=True)
        rows_ref[pl.ds(8 + f, 128, stride=12), :] = jnp.broadcast_to(line, (128, 128))
    send_ref[...] = rows_ref[...].astype(bf16)


def cross_kernel(re_ref, im_ref, after_ref, cross_ref):
    for n in range(16):
        cross_ref[n // 4, 2 * (n % 4)] = re_ref[n]
        cross_ref[n // 4, 2 * (n % 4) + 1] = im_ref[n]


def first_elements(
    recv_ref, vector_ref, coef_ref,
    fac_ref, index_ref, code_ref, kept_ref,
    x_ref, z_ref, w_ref, rows_ref, turned_ref, mode_ref, weight_ref,
):
    rows_ref[...] = recv_ref[...].astype(f32)
    coded = 0.0
    for f, unit in enumerate((1.0, 16.0, 2048.0, 16384.0)):
        coded = coded + unit * rows_ref[pl.ds(8 + f, 128, stride=12), :]
    coded = swap_rows(coded.T).astype(jnp.int32)
    lane = lax.broadcasted_iota(jnp.int32, (128, 128), 1)
    index_ref[...] = 8 * (coded & 15) + (lane & 7)
    mode_ref[...] = (coded >> 4) & 127
    weight_ref[...] = ((coded >> 11) & 7).astype(f32)
    local = (coded >> 14) - 1
    code_ref[...] = jnp.where(local >= 0, 128 * (local & 1) + (lane & 120) + (local >> 1), -1)

    d, r = lax.axis_index("aux"), lax.axis_index("row")
    turned_ref[0:128, :] = vector_ref[...].T
    turned_ref[128:130, :] = coef_ref[...]
    base = pl.multiple_of(32 * (d // 32), 32)
    turned_ref[130:131, :] = turned_ref[pl.ds(32 * r + d % 32, 1), :]

    def factors(v, carry):
        at = pl.ds(pl.multiple_of(8 * v, 8), 8)
        modes, weights = mode_ref[at, :], weight_ref[at, :]
        for q in range(8):
            mode = jnp.broadcast_to(modes[q : q + 1, :], (8, 128))
            weight = weights[q : q + 1, :]
            picked = jnp.take_along_axis(turned_ref[128:136, :], mode, axis=1)
            real, imag, own = picked[0:1, :], picked[1:2, :], picked[2:3, :]
            plus = weight * imag
            minus = jnp.where(weight == 0.0, 1.0, weight * real)
            for e in range(4):
                other = jnp.take_along_axis(turned_ref[pl.ds(base + 8 * e, 8), :], mode, axis=1)
                fac_ref[8 * v + q, 8 * e : 8 * e + 8, :] = plus * (own + other)
                fac_ref[8 * v + q, 32 + 8 * e : 40 + 8 * e, :] = -(minus * (own - other))
        return carry

    lax.fori_loop(0, 16, factors, 0)
    load_elements(x_ref, z_ref, lambda r, k: rows_ref[pl.ds(2 * r + k, 128, stride=12), :])
    couple(x_ref, w_ref, fac_ref, index_ref, code_ref, kept_ref, True)


def send_elements(rows_ref, kept_ref):
    for k in range(8):
        rows_ref[pl.ds(4 * (k // 2) + 2 + k % 2, 128, stride=16), :] = kept_ref[pl.ds(k, 128, stride=8), :]


def first_matrices(cross_ref, kept_ref, energy_ref, rate_ref, send_ref, com_ref, rows_ref):
    state = [jnp.concatenate([cross_ref[r, m] for r in range(4)], axis=0) for m in range(8)]
    result = commutator(state, energy_ref[...], rate_ref)
    for m in range(8):
        com_ref[m] = result[m]
        result[m] = result[m] + repay * rounded_off(state[m])
    store_matrices(rows_ref, result, 0, 16, 4)
    send_elements(rows_ref, kept_ref)
    send_ref[...] = rows_ref[...].astype(bf16)


def next_elements(rows_ref, kept_ref, x_ref, z_ref):
    load_elements(
        x_ref, z_ref,
        lambda r, k: rows_ref[pl.ds(4 * r + k, 128, stride=16), :] + kept_ref[pl.ds(2 * r + k, 128, stride=8), :],
    )


def next_kernel(
    j, recv_ref, com_ref, kept_ref, energy_ref, rate_ref, fac_ref, index_ref, code_ref, *rest
):
    if j > 1:
        total_ref, owed_ref, *rest = rest
    send_ref, com_out, kept_out, total_out, owed_out, x_ref, z_ref, w_ref, rows_ref = rest
    rows_ref[...] = recv_ref[...].astype(f32)
    state = load_matrices(rows_ref, 2, 16, 4)
    state = [state[m] + com_ref[m] for m in range(8)]
    result = commutator(state, energy_ref[...], rate_ref)
    for m in range(8):
        total = weights_of[j - 1] * state[m]
        total_out[m] = total + total_ref[m] if j > 1 else total
        com_out[m] = result[m]
    owed = weights_of[j - 1] * rounded_off(kept_ref[...])
    owed_out[...] = owed + owed_ref[...] if j > 1 else owed
    next_elements(rows_ref, kept_ref, x_ref, z_ref)
    store_matrices(rows_ref, result, 0, 16, 4)
    couple(x_ref, w_ref, fac_ref, index_ref, code_ref, kept_out, False)
    send_elements(rows_ref, kept_out)
    send_ref[...] = rows_ref[...].astype(bf16)


def last_matrices(recv_ref, com_ref, total_ref, energy_ref, rate_ref, cross_ref, rows_ref):
    rows_ref[...] = recv_ref[...].astype(f32)
    state = load_matrices(rows_ref, 2, 16, 4)
    state = [state[m] + com_ref[m] for m in range(8)]
    result = commutator(state, energy_ref[...], rate_ref)
    for m in range(8):
        total = total_ref[m] + weights_of[2] * state[m] + weights_of[3] * result[m]
        for r in range(4):
            cross_ref[r, m] = total[32 * r : 32 * r + 32, :]


def last_elements(
    recv_ref, kept_ref, owed_ref, fac_ref, index_ref, code_ref, after_ref,
    send_ref,
    x_ref, z_ref, w_ref, rows_ref, out_ref,
):
    rows_ref[...] = recv_ref[...].astype(f32)
    next_elements(rows_ref, kept_ref, x_ref, z_ref)
    couple(x_ref, w_ref, fac_ref, index_ref, code_ref, out_ref, False)
    owed = owed_ref[...] + weights_of[2] * rounded_off(kept_ref[...])
    send_ref[...] = (weights_of[3] * out_ref[...] + owed).astype(bf16)


def sum_kernel(re_ref, im_ref, recv_ref, cross_ref, re_out, im_out, rows_ref):
    rows_ref[...] = recv_ref[...].astype(f32)
    for k in range(8):
        parts = swap_blocks(split_rows(rows_ref[pl.ds(k, 128, stride=8), :]))
        for c in range(4):
            n = 2 * k + c // 2
            source, result = ((re_ref, re_out), (im_ref, im_out))[c % 2]
            result[n] = source[n] + (parts[c] + cross_ref[k // 2, 4 * (k % 2) + c])


def vmem():
    return pl.BlockSpec(memory_space=pltpu.VMEM)


def smem():
    return pl.BlockSpec(memory_space=pltpu.SMEM)


def call(kernel, ins, outs, scratch=(), smem_at=(), any_at=()):
    return pl.pallas_call(
        kernel,
        out_shape=[jax.ShapeDtypeStruct(shape, dtype) for shape, dtype in outs],
        in_specs=[
            smem() if i in smem_at else pl.BlockSpec(memory_space=pl.ANY) if i in any_at else vmem() for i in range(len(ins))
        ],
        out_specs=[vmem() for _ in outs],
        scratch_shapes=[pltpu.VMEM(shape, dtype) for shape, dtype in scratch],
        compiler_params=pltpu.CompilerParams(vmem_limit_bytes=40 * 1024 * 1024),
    )(*ins)


lanes = ((128, 128), jnp.int32)
elements = ((16, 64, 128), f32)
terms = ((8, 64, 2048), f32)
matrices = ((8, 128, 128), f32)
messages = ((1024, 128), f32)
both = ((2048, 128), f32)
factors = ((128, 64, 128), f32)
crossing = ((4, 8, 32, 128), f32)


def shards(rho_real, rho_imag, hamiltonian, damping, couplings, mode_vector, mode_coef):
    def to_elements(x, rows):
        return lax.all_to_all(x.reshape(128 * rows // 4, 4, 128), "aux", 0, 0, tiled=True).reshape(128 * rows, 128)

    def along_row(x):
        return lax.all_to_all(x.reshape(4, 256, 128), "row", 0, 0, tiled=True).reshape(4, 8, 32, 128)

    def exchange(x):
        return lax.all_to_all(x.reshape(512, 4, 128), ("aux", "row"), 0, 0, tiled=True).reshape(2048, 128)

    (send,) = call(pack_kernel, (rho_real, rho_imag, couplings), (((1536, 128), bf16),), (((1536, 128), f32),))
    recv = to_elements(send, 12)
    (cross,) = call(cross_kernel, (rho_real, rho_imag, recv), (crossing,), any_at=(2,))
    fac, index, code, kept = call(
        first_elements,
        (recv, mode_vector, mode_coef),
        (factors, lanes, lanes, messages),
        (elements, elements, terms, ((1536, 128), f32), ((136, 128), f32), lanes, ((128, 128), f32)),
    )
    send, com = call(
        first_matrices,
        (along_row(cross), kept, hamiltonian, damping),
        (((2048, 128), bf16), matrices),
        (both,),
        (3,),
    )
    carried = ()
    for j in range(1, 3):
        send, com, kept, *carried = call(
            functools.partial(next_kernel, j),
            (exchange(send), com, kept, hamiltonian, damping, fac, index, code, *carried),
            (((2048, 128), bf16), matrices, messages, matrices, messages),
            (elements, elements, terms, both),
            (4,),
        )
    recv = exchange(send)
    (cross,) = call(
        last_matrices, (recv, com, carried[0], hamiltonian, damping), (crossing,), (both,), (4,)
    )
    (send,) = call(
        last_elements,
        (recv, kept, carried[1], fac, index, code, cross),
        (((1024, 128), bf16),),
        (elements, elements, terms, both, messages),
        any_at=(6,),
    )
    return tuple(
        call(
            sum_kernel,
            (rho_real, rho_imag, to_elements(send, 8), along_row(cross)),
            (((16, 32, 128), f32), ((16, 32, 128), f32)),
            (messages,),
        )
    )


def solution(mesh):
    placed = (
        P("aux", "row", None),
        P("aux", "row", None),
        P(),
        P("aux"),
        P("aux", None, None),
        P(),
        P(),
    )
    return jax.shard_map(
        shards,
        mesh=mesh,
        in_specs=placed,
        out_specs=(P("aux", "row", None), P("aux", "row", None)),
        check_vma=False,
    )
```

```python
import functools

import jax
import jax.numpy as jnp
from jax import lax
from jax.experimental import pallas as pl
from jax.experimental.pallas import tpu as pltpu
from jax.sharding import PartitionSpec as P

step_size = 0.1
weights_of = (step_size, step_size**2 / 2.0, step_size**3 / 6.0, step_size**4 / 24.0)
repay = weights_of[0] / weights_of[1]
high = lax.Precision.HIGHEST
f32 = jnp.float32
bf16 = jnp.bfloat16


def swap_blocks(parts):
    chunk = lax.broadcasted_iota(jnp.int32, (32, 128), 1) // 32
    rows = []
    for j in range(4):
        row = None
        for i in range(4):
            shift = (32 * (i - j)) % 128
            moved = parts[i] if shift == 0 else pltpu.roll(parts[i], shift, 1)
            row = moved if row is None else jnp.where(chunk == i, moved, row)
        rows.append(row)
    return rows


def split_rows(block):
    return [block[32 * j : 32 * j + 32] for j in range(4)]


def commutator(state, energy, rate_ref):
    row = lax.axis_index("row")
    energy = 0.5 * (energy + energy.T)
    result = []
    for n in range(4):
        com = []
        for part in range(2):
            x = state[2 * n + part]
            left = jnp.dot(energy, x, precision=high, preferred_element_type=f32)
            right = jnp.dot(x, energy, precision=high, preferred_element_type=f32)
            com.append(left - right)
        rate = rate_ref[4 * row + n]
        result.append(com[1] - rate * state[2 * n])
        result.append(-com[0] - rate * state[2 * n + 1])
    return result


def load_matrices(rows_ref, first, per_dev, per_row):
    state = [[None] * 4 for _ in range(8)]
    for r in range(4):
        for k in range(2):
            block = rows_ref[pl.ds(per_row * r + first + k, 128, stride=per_dev), :]
            swapped = swap_blocks(split_rows(block))
            for c in range(4):
                state[4 * k + c][r] = swapped[c]
    return [jnp.concatenate(parts, axis=0) for parts in state]


def store_matrices(rows_ref, mats, first, per_dev, per_row):
    for r in range(4):
        for k in range(2):
            parts = [mats[4 * k + c][32 * r : 32 * r + 32, :] for c in range(4)]
            block = jnp.concatenate(swap_blocks(parts), axis=0)
            rows_ref[pl.ds(per_row * r + first + k, 128, stride=per_dev), :] = block


def swap_chunks(parts):
    lane = lax.broadcasted_iota(jnp.int32, (8, 128), 1)
    for s in (1, 2, 4, 8):
        odd = (lane & (8 * s)) != 0
        new = list(parts)
        for i in range(16):
            if not i & s:
                one, two = parts[i], parts[i + s]
                new[i] = jnp.where(odd, pltpu.roll(two, 8 * s, 1), one)
                new[i + s] = jnp.where(odd, two, pltpu.roll(one, 128 - 8 * s, 1))
        parts = new
    return parts


def swap_rows(x):
    lane = lax.broadcasted_iota(jnp.int32, (128, 128), 1)
    row = lax.broadcasted_iota(jnp.int32, (128, 128), 0)
    for s in (1, 2, 4, 8):
        right, low = (lane & (8 * s)) != 0, (row & s) != 0
        ahead = pltpu.roll(pltpu.roll(x, 8 * s, 1), 128 - s, 0)
        behind = pltpu.roll(pltpu.roll(x, 128 - 8 * s, 1), s, 0)
        x = jnp.where(right, jnp.where(low, x, ahead), jnp.where(low, behind, x))
    return x


def load_elements(x_ref, z_ref, rows_of):
    for r in range(4):
        for k in range(2):
            turned = rows_of(r, k).T
            z_ref[4 * r + 2 * k] = turned[:64]
            z_ref[4 * r + 2 * k + 1] = turned[64:]
    for e in range(8):
        at = pl.ds(8 * e, 8)
        for w, part in enumerate(swap_chunks([z_ref[i, at, :] for i in range(16)])):
            x_ref[w, at, :] = part


def couple(x_ref, w_ref, fac_ref, index_ref, code_ref, out_ref, exact):
    target = lax.broadcasted_iota(jnp.int32, (256, 128), 0).astype(f32).astype(bf16)
    for g in range(8):
        index = index_ref[16 * g : 16 * g + 16, :]
        code = code_ref[16 * g : 16 * g + 16, :].astype(f32).astype(bf16)
        for w in range(16):
            row = jnp.broadcast_to(index[w : w + 1, :], (8, 128))
            lanes = pl.ds(128 * w, 128)
            for e in range(4):
                at_re, at_im = pl.ds(8 * e, 8), pl.ds(32 + 8 * e, 8)
                x_re = jnp.take_along_axis(x_ref[w, at_re, :], row, axis=1)
                x_im = jnp.take_along_axis(x_ref[w, at_im, :], row, axis=1)
                fac_re, fac_im = fac_ref[16 * g + w, at_re, :], fac_ref[16 * g + w, at_im, :]
                w_ref[g, at_re, lanes] = fac_re * x_re - fac_im * x_im
                w_ref[g, at_im, lanes] = fac_re * x_im + fac_im * x_re
        term = w_ref[g]
        upper = term.astype(bf16)
        marks = jnp.concatenate(
            [jnp.where(target == code[w : w + 1, :], bf16(1), bf16(0)) for w in range(16)], axis=1
        )
        dims = (((1,), (1,)), ((), ()))
        total = lax.dot_general(marks, upper, dims, preferred_element_type=f32)
        if exact:
            lower = (term - upper.astype(f32)).astype(bf16)
            total = total + lax.dot_general(marks, lower, dims, preferred_element_type=f32)
        out_ref[128 * g : 128 * g + 128, :] = jnp.concatenate([total[:128], total[128:]], axis=1)


def rounded_off(x):
    return x - x.astype(bf16).astype(f32)


def pack_kernel(re_ref, im_ref, couplings_ref, send_ref, own_ref, one_ref, two_ref, three_ref, rows_ref):
    for k in range(8):
        parts = [(re_ref, im_ref)[c % 2][2 * k + c // 2] for c in range(4)]
        rows_ref[pl.ds(k, 128, stride=12), :] = jnp.concatenate(swap_blocks(parts), axis=0)
    lane = lax.broadcasted_iota(jnp.int32, (16, 128), 1)
    source = lax.broadcasted_iota(jnp.int32, (16, 128), 0).astype(f32)
    target, mode, weight = (couplings_ref[f].astype(f32).T for f in range(3))
    fields = [jnp.zeros((16, 128), f32) for _ in range(4)]
    for j in range(6):
        to = jnp.broadcast_to(target[:, j : j + 1], (16, 128)).astype(jnp.int32)
        here = (to // 16) == lane
        values = (
            source,
            jnp.broadcast_to(mode[:, j : j + 1], (16, 128)),
            jnp.broadcast_to(weight[:, j : j + 1], (16, 128)),
            (to % 16 + 1).astype(f32),
        )
        fields = [field + jnp.where(here, value, 0.0) for field, value in zip(fields, values)]
    for f in range(4):
        line = jnp.sum(fields[f], axis=0, keepdims=True)
        rows_ref[pl.ds(8 + f, 128, stride=12), :] = jnp.broadcast_to(line, (128, 128))
    send_ref[...] = rows_ref[...].astype(bf16)
    row = lax.axis_index("row")
    for step, block_ref in enumerate((own_ref, one_ref, two_ref, three_ref)):
        first = 4 * lax.rem(row + step, 4)
        for n in range(4):
            block_ref[2 * n] = re_ref[first + n]
            block_ref[2 * n + 1] = im_ref[first + n]


def first_elements(
    recv_ref, vector_ref, coef_ref, blocks_ref,
    send_ref, fac_out, index_ref, code_ref, kept_ref,
    x_ref, z_ref, w_ref, rows_ref, turned_ref, mode_ref, weight_ref, fac_ref, both_ref, done,
):
    rows_ref[...] = recv_ref[...].astype(f32)
    coded = 0.0
    for f, unit in enumerate((1.0, 16.0, 2048.0, 16384.0)):
        coded = coded + unit * rows_ref[pl.ds(8 + f, 128, stride=12), :]
    coded = swap_rows(coded.T).astype(jnp.int32)
    lane = lax.broadcasted_iota(jnp.int32, (128, 128), 1)
    index_ref[...] = 8 * (coded & 15) + (lane & 7)
    mode_ref[...] = (coded >> 4) & 127
    weight_ref[...] = ((coded >> 11) & 7).astype(f32)
    local = (coded >> 14) - 1
    code_ref[...] = jnp.where(local >= 0, 128 * (local & 1) + (lane & 120) + (local >> 1), -1)

    d, r = lax.axis_index("aux"), lax.axis_index("row")
    turned_ref[0:128, :] = vector_ref[...].T
    turned_ref[128:130, :] = coef_ref[...]
    base = pl.multiple_of(32 * (d // 32), 32)
    turned_ref[130:131, :] = turned_ref[pl.ds(32 * r + d % 32, 1), :]

    def factors(v, carry):
        at = pl.ds(pl.multiple_of(8 * v, 8), 8)
        modes, weights = mode_ref[at, :], weight_ref[at, :]
        for q in range(8):
            mode = jnp.broadcast_to(modes[q : q + 1, :], (8, 128))
            weight = weights[q : q + 1, :]
            picked = jnp.take_along_axis(turned_ref[128:136, :], mode, axis=1)
            real, imag, own = picked[0:1, :], picked[1:2, :], picked[2:3, :]
            plus = weight * imag
            minus = jnp.where(weight == 0.0, 1.0, weight * real)
            for e in range(4):
                other = jnp.take_along_axis(turned_ref[pl.ds(base + 8 * e, 8), :], mode, axis=1)
                fac_ref[8 * v + q, 8 * e : 8 * e + 8, :] = plus * (own + other)
                fac_ref[8 * v + q, 32 + 8 * e : 40 + 8 * e, :] = -(minus * (own - other))
        return carry

    lax.fori_loop(0, 16, factors, 0)
    copy = pltpu.make_async_copy(fac_ref, fac_out, done)
    copy.start()
    load_elements(x_ref, z_ref, lambda r, k: rows_ref[pl.ds(2 * r + k, 128, stride=12), :])
    couple(x_ref, w_ref, fac_ref, index_ref, code_ref, kept_ref, True)
    for r in range(4):
        for k in range(2):
            both_ref[pl.ds(4 * r + k, 128, stride=16), :] = blocks_ref[2 * r + k]
    send_elements(both_ref, kept_ref)
    send_ref[...] = both_ref[...].astype(bf16)
    copy.wait()


def send_elements(rows_ref, kept_ref):
    for k in range(8):
        rows_ref[pl.ds(4 * (k // 2) + 2 + k % 2, 128, stride=16), :] = kept_ref[pl.ds(k, 128, stride=8), :]


def first_matrices(own_ref, one_ref, two_ref, three_ref, energy_ref, rate_ref, com_ref, blocks_ref, whole_ref):
    row = lax.axis_index("row")
    for step, block_ref in enumerate((own_ref, one_ref, two_ref, three_ref)):
        at = pl.ds(pl.multiple_of(32 * lax.rem(row - step + 4, 4), 32), 32)
        for m in range(8):
            whole_ref[m, at, :] = block_ref[m]
    state = [whole_ref[m] for m in range(8)]
    result = commutator(state, energy_ref[...], rate_ref)
    for m in range(8):
        com_ref[m] = result[m]
        result[m] = result[m] + repay * rounded_off(state[m])
    for r in range(4):
        for k in range(2):
            parts = [result[4 * k + c][32 * r : 32 * r + 32, :] for c in range(4)]
            blocks_ref[2 * r + k] = jnp.concatenate(swap_blocks(parts), axis=0)


def next_elements(rows_ref, kept_ref, x_ref, z_ref):
    load_elements(
        x_ref, z_ref,
        lambda r, k: rows_ref[pl.ds(4 * r + k, 128, stride=16), :] + kept_ref[pl.ds(2 * r + k, 128, stride=8), :],
    )


def next_kernel(
    j, recv_ref, com_ref, kept_ref, energy_ref, rate_ref, fac_ref, index_ref, code_ref, *rest
):
    if j > 1:
        total_ref, owed_ref, *rest = rest
    send_ref, com_out, kept_out, total_out, owed_out, x_ref, z_ref, w_ref, rows_ref, held_ref, done = rest
    copy = pltpu.make_async_copy(fac_ref, held_ref, done)
    copy.start()
    rows_ref[...] = recv_ref[...].astype(f32)
    state = load_matrices(rows_ref, 2, 16, 4)
    state = [state[m] + com_ref[m] for m in range(8)]
    result = commutator(state, energy_ref[...], rate_ref)
    for m in range(8):
        total = weights_of[j - 1] * state[m]
        total_out[m] = total + total_ref[m] if j > 1 else total
        com_out[m] = result[m]
    owed = weights_of[j - 1] * rounded_off(kept_ref[...])
    owed_out[...] = owed + owed_ref[...] if j > 1 else owed
    next_elements(rows_ref, kept_ref, x_ref, z_ref)
    store_matrices(rows_ref, result, 0, 16, 4)
    copy.wait()
    couple(x_ref, w_ref, held_ref, index_ref, code_ref, kept_out, False)
    send_elements(rows_ref, kept_out)
    send_ref[...] = rows_ref[...].astype(bf16)


def last_matrices(
    recv_ref, com_ref, total_ref, energy_ref, rate_ref, after_ref, own_ref, one_ref, two_ref, three_ref, rows_ref, whole_ref
):
    rows_ref[...] = recv_ref[...].astype(f32)
    state = load_matrices(rows_ref, 2, 16, 4)
    state = [state[m] + com_ref[m] for m in range(8)]
    result = commutator(state, energy_ref[...], rate_ref)
    for m in range(8):
        total = total_ref[m] + weights_of[2] * state[m] + weights_of[3] * result[m]
        whole_ref[m] = total
    row = lax.axis_index("row")
    for step, block_ref in enumerate((own_ref, one_ref, two_ref, three_ref)):
        at = pl.ds(pl.multiple_of(32 * lax.rem(row + step, 4), 32), 32)
        for m in range(8):
            block_ref[m] = whole_ref[m, at, :]


def last_elements(
    recv_ref, kept_ref, owed_ref, fac_ref, index_ref, code_ref,
    send_ref,
    x_ref, z_ref, w_ref, rows_ref, out_ref, held_ref, done,
):
    copy = pltpu.make_async_copy(fac_ref, held_ref, done)
    copy.start()
    rows_ref[...] = recv_ref[...].astype(f32)
    next_elements(rows_ref, kept_ref, x_ref, z_ref)
    copy.wait()
    couple(x_ref, w_ref, held_ref, index_ref, code_ref, out_ref, False)
    owed = owed_ref[...] + weights_of[2] * rounded_off(kept_ref[...])
    send_ref[...] = (weights_of[3] * out_ref[...] + owed).astype(bf16)


def sum_kernel(
    re_ref, im_ref, recv_ref, own_ref, one_ref, two_ref, three_ref, re_out, im_out, rows_ref, re_sum, im_sum
):
    rows_ref[...] = recv_ref[...].astype(f32)
    for k in range(8):
        parts = swap_blocks(split_rows(rows_ref[pl.ds(k, 128, stride=8), :]))
        for c in range(4):
            (re_sum, im_sum)[c % 2][2 * k + c // 2] = parts[c]
    row = lax.axis_index("row")
    for step, block_ref in enumerate((own_ref, one_ref, two_ref, three_ref)):
        first = 4 * lax.rem(row - step + 4, 4)
        for i in range(4):
            n = first + i
            re_out[n] = re_ref[n] + (re_sum[n] + block_ref[2 * i])
            im_out[n] = im_ref[n] + (im_sum[n] + block_ref[2 * i + 1])


def vmem():
    return pl.BlockSpec(memory_space=pltpu.VMEM)


def smem():
    return pl.BlockSpec(memory_space=pltpu.SMEM)


def call(kernel, ins, outs, scratch=(), smem_at=(), any_at=(), any_out=()):
    return pl.pallas_call(
        kernel,
        out_shape=[jax.ShapeDtypeStruct(shape, dtype) for shape, dtype in outs],
        in_specs=[
            smem() if i in smem_at else pl.BlockSpec(memory_space=pl.ANY) if i in any_at else vmem() for i in range(len(ins))
        ],
        out_specs=[pl.BlockSpec(memory_space=pl.ANY) if i in any_out else vmem() for i in range(len(outs))],
        scratch_shapes=[pltpu.VMEM(*each) if isinstance(each, tuple) else each for each in scratch],
        compiler_params=pltpu.CompilerParams(vmem_limit_bytes=40 * 1024 * 1024),
    )(*ins)


lanes = ((128, 128), jnp.int32)
elements = ((16, 64, 128), f32)
terms = ((8, 64, 2048), f32)
matrices = ((8, 128, 128), f32)
messages = ((1024, 128), f32)
both = ((2048, 128), f32)
factors = ((128, 64, 128), f32)
block = ((8, 32, 128), f32)
copying = pltpu.SemaphoreType.DMA


def shards(rho_real, rho_imag, hamiltonian, damping, couplings, mode_vector, mode_coef):
    def to_elements(x, rows):
        return lax.all_to_all(x.reshape(128 * rows // 4, 4, 128), "aux", 0, 0, tiled=True).reshape(128 * rows, 128)

    def along_row(own, *rest):
        return own, *(
            lax.ppermute(x, "row", [(i, (i + step) % 4) for i in range(4)]) for step, x in enumerate(rest, 1)
        )

    def exchange(x):
        return lax.all_to_all(x.reshape(512, 4, 128), ("aux", "row"), 0, 0, tiled=True).reshape(2048, 128)

    send, *blocks = call(
        pack_kernel,
        (rho_real, rho_imag, jnp.transpose(couplings, (1, 2, 0))),
        (((1536, 128), bf16), block, block, block, block),
        (((1536, 128), f32),),
    )
    recv = to_elements(send, 12)
    com, blocks = call(
        first_matrices,
        (*along_row(*blocks), hamiltonian, damping),
        (matrices, matrices),
        (matrices,),
        (5,),
    )
    send, fac, index, code, kept = call(
        first_elements,
        (recv, mode_vector, mode_coef, blocks),
        (((2048, 128), bf16), factors, lanes, lanes, messages),
        (elements, elements, terms, ((1536, 128), f32), ((136, 128), f32), lanes, ((128, 128), f32), factors, both, copying),
        any_out=(1,),
    )
    carried = ()
    for j in range(1, 3):
        send, com, kept, *carried = call(
            functools.partial(next_kernel, j),
            (exchange(send), com, kept, hamiltonian, damping, fac, index, code, *carried),
            (((2048, 128), bf16), matrices, messages, matrices, messages),
            (elements, elements, terms, both, factors, copying),
            (4,),
            (5,),
        )
    recv = exchange(send)
    (send,) = call(
        last_elements,
        (recv, kept, carried[1], fac, index, code),
        (((1024, 128), bf16),),
        (elements, elements, terms, both, messages, factors, copying),
        any_at=(3,),
    )
    blocks = call(
        last_matrices,
        (recv, com, carried[0], hamiltonian, damping, send),
        (block, block, block, block),
        (both, matrices),
        (4,),
        (5,),
    )
    return tuple(
        call(
            sum_kernel,
            (rho_real, rho_imag, to_elements(send, 8), *along_row(*blocks)),
            (((16, 32, 128), f32), ((16, 32, 128), f32)),
            (messages, ((16, 32, 128), f32), ((16, 32, 128), f32)),
        )
    )


def solution(mesh):
    placed = (
        P("aux", "row", None),
        P("aux", "row", None),
        P(),
        P("aux"),
        P("aux", None, None),
        P(),
        P(),
    )
    return jax.shard_map(
        shards,
        mesh=mesh,
        in_specs=placed,
        out_specs=(P("aux", "row", None), P("aux", "row", None)),
        check_vma=False,
    )
```

```python
import functools

import jax
import jax.numpy as jnp
from jax import lax
from jax.experimental import pallas as pl
from jax.experimental.pallas import tpu as pltpu
from jax.sharding import PartitionSpec as P

step_size = 0.1
weights_of = (step_size, step_size**2 / 2.0, step_size**3 / 6.0, step_size**4 / 24.0)
repay = weights_of[0] / weights_of[1]
high = lax.Precision.HIGHEST
f32 = jnp.float32
bf16 = jnp.bfloat16


def swap_blocks(parts):
    chunk = lax.broadcasted_iota(jnp.int32, (32, 128), 1) // 32
    rows = []
    for j in range(4):
        row = None
        for i in range(4):
            shift = (32 * (i - j)) % 128
            moved = parts[i] if shift == 0 else pltpu.roll(parts[i], shift, 1)
            row = moved if row is None else jnp.where(chunk == i, moved, row)
        rows.append(row)
    return rows


def split_rows(block):
    return [block[32 * j : 32 * j + 32] for j in range(4)]


def commutator(state, fixed_ref):
    energy = fixed_ref[0:128, :]
    result = []
    for n in range(4):
        com = []
        for part in range(2):
            x = state[2 * n + part]
            left = jnp.dot(energy, x, precision=high, preferred_element_type=f32)
            right = jnp.dot(x, energy, precision=high, preferred_element_type=f32)
            com.append(left - right)
        rate = fixed_ref[128 + n : 129 + n, :]
        result.append(com[1] - rate * state[2 * n])
        result.append(-com[0] - rate * state[2 * n + 1])
    return result


def load_matrices(rows_ref, first, per_dev, per_row):
    state = [[None] * 4 for _ in range(8)]
    for r in range(4):
        for k in range(2):
            block = rows_ref[pl.ds(per_row * r + first + k, 128, stride=per_dev), :]
            swapped = swap_blocks(split_rows(block))
            for c in range(4):
                state[4 * k + c][r] = swapped[c]
    return [jnp.concatenate(parts, axis=0) for parts in state]


def store_matrices(rows_ref, mats, first, per_dev, per_row):
    for r in range(4):
        for k in range(2):
            parts = [mats[4 * k + c][32 * r : 32 * r + 32, :] for c in range(4)]
            block = jnp.concatenate(swap_blocks(parts), axis=0)
            rows_ref[pl.ds(per_row * r + first + k, 128, stride=per_dev), :] = block


def swap_rows(x):
    lane = lax.broadcasted_iota(jnp.int32, (128, 128), 1)
    row = lax.broadcasted_iota(jnp.int32, (128, 128), 0)
    for s in (1, 2, 4, 8):
        right, low = (lane & (8 * s)) != 0, (row & s) != 0
        ahead = pltpu.roll(pltpu.roll(x, 8 * s, 1), 128 - s, 0)
        behind = pltpu.roll(pltpu.roll(x, 128 - 8 * s, 1), s, 0)
        x = jnp.where(right, jnp.where(low, x, ahead), jnp.where(low, behind, x))
    return x


def load_elements(x_ref, rows_of):
    left = lax.broadcasted_iota(jnp.int32, (64, 128), 1) < 64
    rows = [rows_of(r, k) for r in range(4) for k in range(2)]
    for w in range(0, 16, 2):
        parts = [row[8 * v : 8 * v + 8, :] for v in (w, w + 1) for row in rows]
        turned = jnp.concatenate(parts, axis=0).T
        even, odd = turned[:64], turned[64:]
        x_ref[w] = jnp.where(left, even, pltpu.roll(odd, 64, 1))
        x_ref[w + 1] = jnp.where(left, pltpu.roll(even, 64, 1), odd)


def couple(x_ref, w_ref, fac_ref, index_ref, code_ref, out_ref, exact):
    target = lax.broadcasted_iota(jnp.int32, (256, 128), 0).astype(f32).astype(bf16)
    for g in range(8):
        index = index_ref[16 * g : 16 * g + 16, :]
        code = code_ref[16 * g : 16 * g + 16, :].astype(f32).astype(bf16)
        for w in range(16):
            row = jnp.broadcast_to(index[w : w + 1, :], (8, 128))
            lanes = pl.ds(128 * w, 128)
            for e in range(4):
                at_re, at_im = pl.ds(8 * e, 8), pl.ds(32 + 8 * e, 8)
                x_re = jnp.take_along_axis(x_ref[w, at_re, :], row, axis=1)
                x_im = jnp.take_along_axis(x_ref[w, at_im, :], row, axis=1)
                fac_re, fac_im = fac_ref[16 * g + w, at_re, :], fac_ref[16 * g + w, at_im, :]
                w_ref[g, at_re, lanes] = fac_re * x_re - fac_im * x_im
                w_ref[g, at_im, lanes] = fac_re * x_im + fac_im * x_re
        term = w_ref[g]
        upper = term.astype(bf16)
        marks = jnp.concatenate(
            [jnp.where(target == code[w : w + 1, :], bf16(1), bf16(0)) for w in range(16)], axis=1
        )
        dims = (((1,), (1,)), ((), ()))
        if exact:
            lower = (term - upper.astype(f32)).astype(bf16)
            total = lax.dot_general(marks, jnp.concatenate([upper, lower], axis=0), dims, preferred_element_type=f32)
            total = total[:, :64] + total[:, 64:]
        else:
            total = lax.dot_general(marks, upper, dims, preferred_element_type=f32)
        out_ref[128 * g : 128 * g + 128, :] = jnp.concatenate([total[:128], total[128:]], axis=1)


def rounded_off(x):
    return x - x.astype(bf16).astype(f32)


def pack_kernel(
    re_at, im_at, couplings_at,
    send_ref, own_ref, one_ref, two_ref, three_ref,
    rows_ref, re_ref, im_ref, couplings_ref, done_re, done_im, done_couplings,
):
    copies = [
        pltpu.make_async_copy(couplings_at, couplings_ref, done_couplings),
        pltpu.make_async_copy(re_at, re_ref, done_re),
        pltpu.make_async_copy(im_at, im_ref, done_im),
    ]
    for copy in copies:
        copy.start()
    copies[0].wait()
    lane = lax.broadcasted_iota(jnp.int32, (16, 128), 1)
    source = lax.broadcasted_iota(jnp.int32, (16, 128), 0).astype(f32)
    target, mode, weight = (couplings_ref[f].astype(f32).T for f in range(3))
    fields = [jnp.zeros((16, 128), f32) for _ in range(4)]
    for j in range(6):
        to = jnp.broadcast_to(target[:, j : j + 1], (16, 128)).astype(jnp.int32)
        here = (to // 16) == lane
        values = (
            source,
            jnp.broadcast_to(mode[:, j : j + 1], (16, 128)),
            jnp.broadcast_to(weight[:, j : j + 1], (16, 128)),
            (to % 16 + 1).astype(f32),
        )
        fields = [field + jnp.where(here, value, 0.0) for field, value in zip(fields, values)]
    copies[1].wait()
    copies[2].wait()
    for k in range(8):
        parts = [(re_ref, im_ref)[c % 2][2 * k + c // 2] for c in range(4)]
        rows_ref[pl.ds(k, 128, stride=12), :] = jnp.concatenate(swap_blocks(parts), axis=0)
    for f in range(4):
        line = jnp.sum(fields[f], axis=0, keepdims=True)
        rows_ref[pl.ds(8 + f, 128, stride=12), :] = jnp.broadcast_to(line, (128, 128))
    send_ref[...] = rows_ref[...].astype(bf16)
    row = lax.axis_index("row")
    for step, block_ref in enumerate((own_ref, one_ref, two_ref, three_ref)):
        first = 4 * lax.rem(row + step, 4)
        for n in range(4):
            block_ref[2 * n] = re_ref[first + n]
            block_ref[2 * n + 1] = im_ref[first + n]


def first_elements(
    recv_ref, turned_ref, blocks_ref,
    send_ref, fac_ref, index_ref, code_ref, kept_ref,
    x_ref, w_ref, rows_ref, mode_ref, weight_ref, both_ref,
):
    rows_ref[...] = recv_ref[...].astype(f32)
    coded = 0.0
    for f, unit in enumerate((1.0, 16.0, 2048.0, 16384.0)):
        coded = coded + unit * rows_ref[pl.ds(8 + f, 128, stride=12), :]
    coded = swap_rows(coded.T).astype(jnp.int32)
    lane = lax.broadcasted_iota(jnp.int32, (128, 128), 1)
    index_ref[...] = 64 * (coded & 1) + 8 * ((coded >> 1) & 7) + (lane & 7)
    mode_ref[...] = (coded >> 4) & 127
    weight_ref[...] = ((coded >> 11) & 7).astype(f32)
    local = (coded >> 14) - 1
    code_ref[...] = jnp.where(local >= 0, 128 * (local & 1) + (lane & 120) + (local >> 1), -1)

    base = pl.multiple_of(32 * (lax.axis_index("aux") // 32), 32)

    def factors(v, carry):
        at = pl.ds(pl.multiple_of(8 * v, 8), 8)
        modes, weights = mode_ref[at, :], weight_ref[at, :]
        for q in range(8):
            mode = jnp.broadcast_to(modes[q : q + 1, :], (8, 128))
            weight = weights[q : q + 1, :]
            picked = jnp.take_along_axis(turned_ref[128:136, :], mode, axis=1)
            real, imag, own = picked[0:1, :], picked[1:2, :], picked[2:3, :]
            plus = weight * imag
            minus = jnp.where(weight == 0.0, 1.0, weight * real)
            for e in range(4):
                other = jnp.take_along_axis(turned_ref[pl.ds(base + 8 * e, 8), :], mode, axis=1)
                fac_ref[8 * v + q, 8 * e : 8 * e + 8, :] = plus * (own + other)
                fac_ref[8 * v + q, 32 + 8 * e : 40 + 8 * e, :] = -(minus * (own - other))
        return carry

    lax.fori_loop(0, 16, factors, 0, unroll=2)
    load_elements(x_ref, lambda r, k: rows_ref[pl.ds(2 * r + k, 128, stride=12), :])
    couple(x_ref, w_ref, fac_ref, index_ref, code_ref, kept_ref, True)
    for r in range(4):
        for k in range(2):
            both_ref[pl.ds(4 * r + k, 128, stride=16), :] = blocks_ref[2 * r + k]
    send_elements(both_ref, kept_ref)
    send_ref[...] = both_ref[...].astype(bf16)


def send_elements(rows_ref, kept_ref):
    for k in range(8):
        rows_ref[pl.ds(4 * (k // 2) + 2 + k % 2, 128, stride=16), :] = kept_ref[pl.ds(k, 128, stride=8), :]


def first_matrices(
    own_ref, one_ref, two_ref, three_ref, energy_ref, vector_ref, coef_ref, rate_ref,
    com_ref, blocks_ref, fixed_ref, turned_ref,
    whole_ref,
):
    d, row = lax.axis_index("aux"), lax.axis_index("row")
    fixed_ref[0:128, :] = 0.5 * (energy_ref[...] + energy_ref[...].T)
    for n in range(4):
        fixed_ref[128 + n : 129 + n, :] = jnp.full((1, 128), rate_ref[4 * row + n], f32)
    fixed_ref[132:136, :] = jnp.zeros((4, 128), f32)
    turned_ref[0:128, :] = vector_ref[...].T
    turned_ref[128:130, :] = coef_ref[...]
    turned_ref[130:131, :] = turned_ref[pl.ds(32 * row + d % 32, 1), :]
    turned_ref[131:136, :] = jnp.zeros((5, 128), f32)
    for step, block_ref in enumerate((own_ref, one_ref, two_ref, three_ref)):
        at = pl.ds(pl.multiple_of(32 * lax.rem(row - step + 4, 4), 32), 32)
        for m in range(8):
            whole_ref[m, at, :] = block_ref[m]
    state = [whole_ref[m] for m in range(8)]
    result = commutator(state, fixed_ref)
    for m in range(8):
        com_ref[m] = result[m]
        result[m] = result[m] + repay * rounded_off(state[m])
    for r in range(4):
        for k in range(2):
            parts = [result[4 * k + c][32 * r : 32 * r + 32, :] for c in range(4)]
            blocks_ref[2 * r + k] = jnp.concatenate(swap_blocks(parts), axis=0)


def next_elements(rows_ref, kept_ref, x_ref):
    load_elements(
        x_ref,
        lambda r, k: rows_ref[pl.ds(4 * r + k, 128, stride=16), :] + kept_ref[pl.ds(2 * r + k, 128, stride=8), :],
    )


def next_kernel(
    j, recv_ref, com_ref, kept_ref, fixed_ref, fac_ref, index_ref, code_ref, *rest
):
    if j > 1:
        total_ref, owed_ref, *rest = rest
    send_ref, com_out, kept_out, total_out, owed_out, x_ref, w_ref, rows_ref = rest
    rows_ref[...] = recv_ref[...].astype(f32)
    state = load_matrices(rows_ref, 2, 16, 4)
    state = [state[m] + com_ref[m] for m in range(8)]
    result = commutator(state, fixed_ref)
    for m in range(8):
        total = weights_of[j - 1] * state[m]
        total_out[m] = total + total_ref[m] if j > 1 else total
        com_out[m] = result[m]
    owed = weights_of[j - 1] * rounded_off(kept_ref[...])
    owed_out[...] = owed + owed_ref[...] if j > 1 else owed
    next_elements(rows_ref, kept_ref, x_ref)
    store_matrices(rows_ref, result, 0, 16, 4)
    couple(x_ref, w_ref, fac_ref, index_ref, code_ref, kept_out, False)
    send_elements(rows_ref, kept_out)
    send_ref[...] = rows_ref[...].astype(bf16)


def last_matrices(
    recv_ref, com_ref, total_ref, fixed_ref, after_ref, own_ref, one_ref, two_ref, three_ref, rows_ref, whole_ref
):
    rows_ref[...] = recv_ref[...].astype(f32)
    state = load_matrices(rows_ref, 2, 16, 4)
    state = [state[m] + com_ref[m] for m in range(8)]
    result = commutator(state, fixed_ref)
    for m in range(8):
        total = total_ref[m] + weights_of[2] * state[m] + weights_of[3] * result[m]
        whole_ref[m] = total
    row = lax.axis_index("row")
    for step, block_ref in enumerate((own_ref, one_ref, two_ref, three_ref)):
        at = pl.ds(pl.multiple_of(32 * lax.rem(row + step, 4), 32), 32)
        for m in range(8):
            block_ref[m] = whole_ref[m, at, :]


def last_elements(
    recv_ref, kept_ref, owed_ref, fac_ref, index_ref, code_ref,
    send_ref,
    x_ref, w_ref, rows_ref, out_ref,
):
    rows_ref[...] = recv_ref[...].astype(f32)
    next_elements(rows_ref, kept_ref, x_ref)
    couple(x_ref, w_ref, fac_ref, index_ref, code_ref, out_ref, False)
    owed = owed_ref[...] + weights_of[2] * rounded_off(kept_ref[...])
    send_ref[...] = (weights_of[3] * out_ref[...] + owed).astype(bf16)


def sum_kernel(
    re_ref, im_ref, recv_ref, own_ref, one_ref, two_ref, three_ref, re_out, im_out, rows_ref, re_sum, im_sum
):
    rows_ref[...] = recv_ref[...].astype(f32)
    for k in range(8):
        parts = swap_blocks(split_rows(rows_ref[pl.ds(k, 128, stride=8), :]))
        for c in range(4):
            (re_sum, im_sum)[c % 2][2 * k + c // 2] = parts[c]
    row = lax.axis_index("row")
    for step, block_ref in enumerate((own_ref, one_ref, two_ref, three_ref)):
        first = 4 * lax.rem(row - step + 4, 4)
        for i in range(4):
            n = first + i
            re_out[n] = re_ref[n] + (re_sum[n] + block_ref[2 * i])
            im_out[n] = im_ref[n] + (im_sum[n] + block_ref[2 * i + 1])


def vmem():
    return pl.BlockSpec(memory_space=pltpu.VMEM)


def smem():
    return pl.BlockSpec(memory_space=pltpu.SMEM)


def call(kernel, ins, outs, scratch=(), smem_at=(), any_at=(), room=24):
    return pl.pallas_call(
        kernel,
        out_shape=[jax.ShapeDtypeStruct(shape, dtype) for shape, dtype in outs],
        in_specs=[
            smem() if i in smem_at else pl.BlockSpec(memory_space=pl.ANY) if i in any_at else vmem() for i in range(len(ins))
        ],
        out_specs=[vmem() for _ in outs],
        scratch_shapes=[pltpu.VMEM(*each) if isinstance(each, tuple) else each for each in scratch],
        compiler_params=pltpu.CompilerParams(vmem_limit_bytes=room * 1024 * 1024),
    )(*ins)


lanes = ((128, 128), jnp.int32)
elements = ((16, 64, 128), f32)
terms = ((8, 64, 2048), f32)
matrices = ((8, 128, 128), f32)
messages = ((1024, 128), f32)
both = ((2048, 128), f32)
factors = ((128, 64, 128), f32)
block = ((8, 32, 128), f32)
constants = ((136, 128), f32)
part = ((16, 32, 128), f32)
copying = pltpu.SemaphoreType.DMA


def shards(rho_real, rho_imag, hamiltonian, damping, couplings, mode_vector, mode_coef):
    def to_elements(x, rows):
        return lax.all_to_all(x.reshape(128 * rows // 4, 4, 128), "aux", 0, 0, tiled=True).reshape(128 * rows, 128)

    def along_row(own, *rest):
        return own, *(
            lax.ppermute(x, "row", [(i, (i + step) % 4) for i in range(4)]) for step, x in enumerate(rest, 1)
        )

    def exchange(x):
        return lax.all_to_all(x.reshape(512, 4, 128), ("aux", "row"), 0, 0, tiled=True).reshape(2048, 128)

    send, *blocks = call(
        pack_kernel,
        (rho_real, rho_imag, jnp.transpose(couplings, (1, 2, 0))),
        (((1536, 128), bf16), block, block, block, block),
        (((1536, 128), f32), part, part, ((3, 6, 16), jnp.int32), copying, copying, copying),
        any_at=(0, 1, 2),
        room=60,
    )
    recv = to_elements(send, 12)
    com, blocks, fixed, turned = call(
        first_matrices,
        (*along_row(*blocks), hamiltonian, mode_vector, mode_coef, damping),
        (matrices, matrices, constants, constants),
        (matrices,),
        (7,),
    )
    send, fac, index, code, kept = call(
        first_elements,
        (recv, turned, blocks),
        (((2048, 128), bf16), factors, lanes, lanes, messages),
        (elements, terms, ((1536, 128), f32), lanes, ((128, 128), f32), both),
    )
    carried = ()
    for j in range(1, 3):
        send, com, kept, *carried = call(
            functools.partial(next_kernel, j),
            (exchange(send), com, kept, fixed, fac, index, code, *carried),
            (((2048, 128), bf16), matrices, messages, matrices, messages),
            (elements, terms, both),
        )
    recv = exchange(send)
    (send,) = call(
        last_elements,
        (recv, kept, carried[1], fac, index, code),
        (((1024, 128), bf16),),
        (elements, terms, both, messages),
    )
    blocks = call(
        last_matrices,
        (recv, com, carried[0], fixed, send),
        (block, block, block, block),
        (both, matrices),
        any_at=(4,),
    )
    return tuple(
        call(
            sum_kernel,
            (rho_real, rho_imag, to_elements(send, 8), *along_row(*blocks)),
            (part, part),
            (messages, part, part),
        )
    )


def solution(mesh):
    placed = (
        P("aux", "row", None),
        P("aux", "row", None),
        P(),
        P("aux"),
        P("aux", None, None),
        P(),
        P(),
    )
    return jax.shard_map(
        shards,
        mesh=mesh,
        in_specs=placed,
        out_specs=(P("aux", "row", None), P("aux", "row", None)),
        check_vma=False,
    )
```

```python
import functools

import jax
import jax.numpy as jnp
from jax import lax
from jax.experimental import pallas as pl
from jax.experimental.pallas import tpu as pltpu
from jax.sharding import PartitionSpec as P

step_size = 0.1
weights_of = (step_size, step_size**2 / 2.0, step_size**3 / 6.0, step_size**4 / 24.0)
repay = weights_of[0] / weights_of[1]
high = lax.Precision.HIGHEST
f32 = jnp.float32
bf16 = jnp.bfloat16


def swap_blocks(parts):
    chunk = lax.broadcasted_iota(jnp.int32, (32, 128), 1) // 32
    rows = []
    for j in range(4):
        row = None
        for i in range(4):
            shift = (32 * (i - j)) % 128
            moved = parts[i] if shift == 0 else pltpu.roll(parts[i], shift, 1)
            row = moved if row is None else jnp.where(chunk == i, moved, row)
        rows.append(row)
    return rows


def split_rows(block):
    return [block[32 * j : 32 * j + 32] for j in range(4)]


def commutator(state, fixed_ref):
    energy = fixed_ref[0:128, :]
    result = []
    for n in range(4):
        com = []
        for part in range(2):
            x = state[2 * n + part]
            left = jnp.dot(energy, x, precision=high, preferred_element_type=f32)
            right = jnp.dot(x, energy, precision=high, preferred_element_type=f32)
            com.append(left - right)
        rate = fixed_ref[128 + n : 129 + n, :]
        result.append(com[1] - rate * state[2 * n])
        result.append(-com[0] - rate * state[2 * n + 1])
    return result


def load_matrices(rows_ref, first, per_dev, per_row):
    state = [[None] * 4 for _ in range(8)]
    for r in range(4):
        for k in range(2):
            block = rows_ref[pl.ds(per_row * r + first + k, 128, stride=per_dev), :]
            swapped = swap_blocks(split_rows(block))
            for c in range(4):
                state[4 * k + c][r] = swapped[c]
    return [jnp.concatenate(parts, axis=0) for parts in state]


def store_matrices(rows_ref, mats, first, per_dev, per_row):
    for r in range(4):
        for k in range(2):
            parts = [mats[4 * k + c][32 * r : 32 * r + 32, :] for c in range(4)]
            block = jnp.concatenate(swap_blocks(parts), axis=0)
            rows_ref[pl.ds(per_row * r + first + k, 128, stride=per_dev), :] = block


def swap_rows(x):
    lane = lax.broadcasted_iota(jnp.int32, (128, 128), 1)
    row = lax.broadcasted_iota(jnp.int32, (128, 128), 0)
    for s in (1, 2, 4, 8):
        right, low = (lane & (8 * s)) != 0, (row & s) != 0
        ahead = pltpu.roll(pltpu.roll(x, 8 * s, 1), 128 - s, 0)
        behind = pltpu.roll(pltpu.roll(x, 128 - 8 * s, 1), s, 0)
        x = jnp.where(right, jnp.where(low, x, ahead), jnp.where(low, behind, x))
    return x


def load_elements(x_ref, rows_of):
    left = lax.broadcasted_iota(jnp.int32, (64, 128), 1) < 64
    rows = [rows_of(r, k) for r in range(4) for k in range(2)]
    for w in range(0, 16, 2):
        parts = [row[8 * v : 8 * v + 8, :] for v in (w, w + 1) for row in rows]
        turned = jnp.concatenate(parts, axis=0).T
        even, odd = turned[:64], turned[64:]
        x_ref[w] = jnp.where(left, even, pltpu.roll(odd, 64, 1))
        x_ref[w + 1] = jnp.where(left, pltpu.roll(even, 64, 1), odd)


def couple(x_ref, w_ref, fac_ref, index_ref, code_ref, out_ref):
    target = lax.broadcasted_iota(jnp.int32, (256, 128), 0).astype(f32).astype(bf16)
    for g in range(8):
        index = index_ref[16 * g : 16 * g + 16, :]
        code = code_ref[16 * g : 16 * g + 16, :].astype(f32).astype(bf16)
        for w in range(16):
            row = jnp.broadcast_to(index[w : w + 1, :], (8, 128))
            lanes = pl.ds(128 * w, 128)
            for e in range(4):
                at_re, at_im = pl.ds(8 * e, 8), pl.ds(32 + 8 * e, 8)
                x_re = jnp.take_along_axis(x_ref[w, at_re, :], row, axis=1)
                x_im = jnp.take_along_axis(x_ref[w, at_im, :], row, axis=1)
                fac_re, fac_im = fac_ref[16 * g + w, at_re, :], fac_ref[16 * g + w, at_im, :]
                w_ref[g, at_re, lanes] = fac_re * x_re - fac_im * x_im
                w_ref[g, at_im, lanes] = fac_re * x_im + fac_im * x_re
        term = w_ref[g]
        upper = term.astype(bf16)
        marks = jnp.concatenate(
            [jnp.where(target == code[w : w + 1, :], bf16(1), bf16(0)) for w in range(16)], axis=1
        )
        dims = (((1,), (1,)), ((), ()))
        lower = (term - upper.astype(f32)).astype(bf16)
        total = lax.dot_general(marks, jnp.concatenate([upper, lower], axis=0), dims, preferred_element_type=f32)
        total = total[:, :64] + total[:, 64:]
        out_ref[128 * g : 128 * g + 128, :] = jnp.concatenate([total[:128], total[128:]], axis=1)


def rounded_off(x):
    return x - x.astype(bf16).astype(f32)


def pack_kernel(
    re_at, im_at, couplings_at,
    send_ref, own_at, one_at, two_at, three_at,
    rows_ref, re_ref, im_ref, couplings_ref, done,
):
    halves = [pl.ds(0, 8), pl.ds(8, 8)]
    loads = [pltpu.make_async_copy(couplings_at, couplings_ref, done.at[0])]
    for h, half in enumerate(halves):
        loads.append(pltpu.make_async_copy(re_at.at[half], re_ref.at[half], done.at[1 + 2 * h]))
        loads.append(pltpu.make_async_copy(im_at.at[half], im_ref.at[half], done.at[2 + 2 * h]))
    row = lax.axis_index("row")
    blocks = []
    for step, block_at in enumerate((own_at, one_at, two_at, three_at)):
        four = pl.ds(4 * lax.rem(row + step, 4), 4)
        blocks.append(pltpu.make_async_copy(re_at.at[four], block_at.at[pl.ds(0, 4)], done.at[5 + 2 * step]))
        blocks.append(pltpu.make_async_copy(im_at.at[four], block_at.at[pl.ds(4, 4)], done.at[6 + 2 * step]))
    for copy in loads + blocks:
        copy.start()
    loads[0].wait()
    lane = lax.broadcasted_iota(jnp.int32, (16, 128), 1)
    source = lax.broadcasted_iota(jnp.int32, (16, 128), 0).astype(f32)
    target, mode, weight = (couplings_ref[f].astype(f32).T for f in range(3))
    fields = [jnp.zeros((16, 128), f32) for _ in range(4)]
    for j in range(6):
        to = jnp.broadcast_to(target[:, j : j + 1], (16, 128)).astype(jnp.int32)
        here = (to // 16) == lane
        values = (
            source,
            jnp.broadcast_to(mode[:, j : j + 1], (16, 128)),
            jnp.broadcast_to(weight[:, j : j + 1], (16, 128)),
            (to % 16 + 1).astype(f32),
        )
        fields = [field + jnp.where(here, value, 0.0) for field, value in zip(fields, values)]
    for f in range(4):
        line = jnp.sum(fields[f], axis=0, keepdims=True)
        rows_ref[pl.ds(8 + f, 128, stride=12), :] = jnp.broadcast_to(line, (128, 128))
    for k in range(8):
        if k % 4 == 0:
            loads[1 + k // 2].wait()
            loads[2 + k // 2].wait()
        parts = [(re_ref, im_ref)[c % 2][2 * k + c // 2] for c in range(4)]
        rows_ref[pl.ds(k, 128, stride=12), :] = jnp.concatenate(swap_blocks(parts), axis=0)
    send_ref[...] = rows_ref[...].astype(bf16)
    for copy in blocks:
        copy.wait()


def first_elements(
    recv_ref, turned_ref, blocks_ref,
    send_ref, fac_ref, index_ref, code_ref, kept_ref,
    x_ref, w_ref, rows_ref, mode_ref, weight_ref, both_ref,
):
    rows_ref[...] = recv_ref[...].astype(f32)
    coded = 0.0
    for f, unit in enumerate((1.0, 16.0, 2048.0, 16384.0)):
        coded = coded + unit * rows_ref[pl.ds(8 + f, 128, stride=12), :]
    coded = swap_rows(coded.T).astype(jnp.int32)
    lane = lax.broadcasted_iota(jnp.int32, (128, 128), 1)
    index_ref[...] = 64 * (coded & 1) + 8 * ((coded >> 1) & 7) + (lane & 7)
    mode_ref[...] = (coded >> 4) & 127
    weight_ref[...] = ((coded >> 11) & 7).astype(f32)
    local = (coded >> 14) - 1
    code_ref[...] = jnp.where(local >= 0, 128 * (local & 1) + (lane & 120) + (local >> 1), -1)

    base = pl.multiple_of(32 * (lax.axis_index("aux") // 32), 32)

    def factors(v, carry):
        at = pl.ds(pl.multiple_of(8 * v, 8), 8)
        modes, weights = mode_ref[at, :], weight_ref[at, :]
        for q in range(8):
            mode = jnp.broadcast_to(modes[q : q + 1, :], (8, 128))
            weight = weights[q : q + 1, :]
            picked = jnp.take_along_axis(turned_ref[128:136, :], mode, axis=1)
            real, imag, own = picked[0:1, :], picked[1:2, :], picked[2:3, :]
            plus = weight * imag
            minus = jnp.where(weight == 0.0, 1.0, weight * real)
            for e in range(4):
                other = jnp.take_along_axis(turned_ref[pl.ds(base + 8 * e, 8), :], mode, axis=1)
                fac_ref[8 * v + q, 8 * e : 8 * e + 8, :] = plus * (own + other)
                fac_ref[8 * v + q, 32 + 8 * e : 40 + 8 * e, :] = -(minus * (own - other))
        return carry

    lax.fori_loop(0, 16, factors, 0, unroll=2)
    load_elements(x_ref, lambda r, k: rows_ref[pl.ds(2 * r + k, 128, stride=12), :])
    couple(x_ref, w_ref, fac_ref, index_ref, code_ref, kept_ref)
    for r in range(4):
        for k in range(2):
            both_ref[pl.ds(4 * r + k, 128, stride=16), :] = blocks_ref[2 * r + k]
    send_elements(both_ref, kept_ref)
    send_ref[...] = both_ref[...].astype(bf16)


def send_elements(rows_ref, kept_ref):
    for k in range(8):
        rows_ref[pl.ds(4 * (k // 2) + 2 + k % 2, 128, stride=16), :] = kept_ref[pl.ds(k, 128, stride=8), :]


def first_matrices(
    own_ref, one_ref, two_ref, three_ref, given_ref,
    com_ref, blocks_ref, fixed_ref, turned_ref,
    whole_ref,
):
    d, row = lax.axis_index("aux"), lax.axis_index("row")
    energy = given_ref[0:128, :]
    fixed_ref[0:128, :] = 0.5 * (energy + energy.T)
    lane = lax.broadcasted_iota(jnp.int32, (1, 128), 1)
    for n in range(4):
        rate = jnp.sum(jnp.where(lane == 4 * row + n, given_ref[258:259, :], 0.0), axis=1, keepdims=True)
        fixed_ref[128 + n : 129 + n, :] = jnp.broadcast_to(rate, (1, 128))
    fixed_ref[132:136, :] = jnp.zeros((4, 128), f32)
    turned_ref[0:128, :] = given_ref[128:256, :].T
    turned_ref[128:130, :] = given_ref[256:258, :]
    turned_ref[130:131, :] = turned_ref[pl.ds(32 * row + d % 32, 1), :]
    turned_ref[131:136, :] = jnp.zeros((5, 128), f32)
    for step, block_ref in enumerate((own_ref, one_ref, two_ref, three_ref)):
        at = pl.ds(pl.multiple_of(32 * lax.rem(row - step + 4, 4), 32), 32)
        for m in range(8):
            whole_ref[m, at, :] = block_ref[4 * (m % 2) + m // 2]
    state = [whole_ref[m] for m in range(8)]
    result = commutator(state, fixed_ref)
    for m in range(8):
        com_ref[m] = result[m]
        result[m] = result[m] + repay * rounded_off(state[m])
    for r in range(4):
        for k in range(2):
            parts = [result[4 * k + c][32 * r : 32 * r + 32, :] for c in range(4)]
            blocks_ref[2 * r + k] = jnp.concatenate(swap_blocks(parts), axis=0)


def next_elements(rows_ref, kept_ref, x_ref):
    load_elements(
        x_ref,
        lambda r, k: rows_ref[pl.ds(4 * r + k, 128, stride=16), :] + kept_ref[pl.ds(2 * r + k, 128, stride=8), :],
    )


def next_kernel(
    j, recv_ref, com_ref, kept_ref, fixed_ref, fac_ref, index_ref, code_ref, *rest
):
    if j > 1:
        total_ref, owed_ref, *rest = rest
    send_ref, com_out, kept_out, total_out, owed_out, x_ref, w_ref, rows_ref = rest
    rows_ref[...] = recv_ref[...].astype(f32)
    state = load_matrices(rows_ref, 2, 16, 4)
    state = [state[m] + com_ref[m] for m in range(8)]
    result = commutator(state, fixed_ref)
    for m in range(8):
        total = weights_of[j - 1] * state[m]
        total_out[m] = total + total_ref[m] if j > 1 else total
        com_out[m] = result[m]
    owed = weights_of[j - 1] * rounded_off(kept_ref[...])
    owed_out[...] = owed + owed_ref[...] if j > 1 else owed
    next_elements(rows_ref, kept_ref, x_ref)
    store_matrices(rows_ref, result, 0, 16, 4)
    couple(x_ref, w_ref, fac_ref, index_ref, code_ref, kept_out)
    send_elements(rows_ref, kept_out)
    send_ref[...] = rows_ref[...].astype(bf16)


def last_matrices(
    recv_ref, com_ref, total_ref, fixed_ref, after_ref, own_ref, one_ref, two_ref, three_ref, rows_ref, whole_ref
):
    rows_ref[...] = recv_ref[...].astype(f32)
    state = load_matrices(rows_ref, 2, 16, 4)
    state = [state[m] + com_ref[m] for m in range(8)]
    result = commutator(state, fixed_ref)
    for m in range(8):
        total = total_ref[m] + weights_of[2] * state[m] + weights_of[3] * result[m]
        whole_ref[m] = total
    row = lax.axis_index("row")
    for step, block_ref in enumerate((own_ref, one_ref, two_ref, three_ref)):
        at = pl.ds(pl.multiple_of(32 * lax.rem(row + step, 4), 32), 32)
        for m in range(8):
            block_ref[m] = whole_ref[m, at, :]


def last_elements(
    recv_ref, kept_ref, owed_ref, fac_ref, index_ref, code_ref,
    send_ref,
    x_ref, w_ref, rows_ref, out_ref,
):
    rows_ref[...] = recv_ref[...].astype(f32)
    next_elements(rows_ref, kept_ref, x_ref)
    couple(x_ref, w_ref, fac_ref, index_ref, code_ref, out_ref)
    owed = owed_ref[...] + weights_of[2] * rounded_off(kept_ref[...])
    send_ref[...] = (weights_of[3] * out_ref[...] + owed).astype(bf16)


def sum_kernel(
    re_ref, im_ref, recv_ref, own_ref, one_ref, two_ref, three_ref, re_out, im_out, rows_ref, re_sum, im_sum
):
    rows_ref[...] = recv_ref[...].astype(f32)
    for k in range(8):
        parts = swap_blocks(split_rows(rows_ref[pl.ds(k, 128, stride=8), :]))
        for c in range(4):
            (re_sum, im_sum)[c % 2][2 * k + c // 2] = parts[c]
    row = lax.axis_index("row")
    for step, block_ref in enumerate((own_ref, one_ref, two_ref, three_ref)):
        first = 4 * lax.rem(row - step + 4, 4)
        for i in range(4):
            n = first + i
            re_out[n] = re_ref[n] + (re_sum[n] + block_ref[2 * i])
            im_out[n] = im_ref[n] + (im_sum[n] + block_ref[2 * i + 1])


def vmem():
    return pl.BlockSpec(memory_space=pltpu.VMEM)


def smem():
    return pl.BlockSpec(memory_space=pltpu.SMEM)


def call(kernel, ins, outs, scratch=(), smem_at=(), any_at=(), any_out=(), room=24):
    return pl.pallas_call(
        kernel,
        out_shape=[jax.ShapeDtypeStruct(shape, dtype) for shape, dtype in outs],
        in_specs=[
            smem() if i in smem_at else pl.BlockSpec(memory_space=pl.ANY) if i in any_at else vmem() for i in range(len(ins))
        ],
        out_specs=[pl.BlockSpec(memory_space=pl.ANY) if i in any_out else vmem() for i in range(len(outs))],
        scratch_shapes=[pltpu.VMEM(*each) if isinstance(each, tuple) else each for each in scratch],
        compiler_params=pltpu.CompilerParams(vmem_limit_bytes=room * 1024 * 1024),
    )(*ins)


lanes = ((128, 128), jnp.int32)
elements = ((16, 64, 128), f32)
terms = ((8, 64, 2048), f32)
matrices = ((8, 128, 128), f32)
messages = ((1024, 128), f32)
both = ((2048, 128), f32)
factors = ((128, 64, 128), f32)
block = ((8, 32, 128), f32)
constants = ((136, 128), f32)
part = ((16, 32, 128), f32)


def shards(rho_real, rho_imag, hamiltonian, damping, couplings, mode_vector, mode_coef):
    def to_elements(x, rows):
        return lax.all_to_all(x.reshape(128 * rows // 4, 4, 128), "aux", 0, 0, tiled=True).reshape(128 * rows, 128)

    def along_row(own, *rest):
        return own, *(
            lax.ppermute(x, "row", [(i, (i + step) % 4) for i in range(4)]) for step, x in enumerate(rest, 1)
        )

    def exchange(x):
        return lax.all_to_all(x.reshape(512, 4, 128), ("aux", "row"), 0, 0, tiled=True).reshape(2048, 128)

    send, *blocks = call(
        pack_kernel,
        (rho_real, rho_imag, jnp.transpose(couplings, (1, 2, 0))),
        (((1536, 128), bf16), block, block, block, block),
        (((1536, 128), f32), part, part, ((3, 6, 16), jnp.int32), pltpu.SemaphoreType.DMA((13,))),
        any_at=(0, 1, 2),
        any_out=(1, 2, 3, 4),
        room=60,
    )
    recv = to_elements(send, 12)
    last_rows = jnp.pad(damping[None], ((0, 5), (0, 112)))
    given = jnp.concatenate([hamiltonian, mode_vector, mode_coef, last_rows], axis=0)
    com, blocks, fixed, turned = call(
        first_matrices,
        (*along_row(*blocks), given),
        (matrices, matrices, constants, constants),
        (matrices,),
    )
    send, fac, index, code, kept = call(
        first_elements,
        (recv, turned, blocks),
        (((2048, 128), bf16), factors, lanes, lanes, messages),
        (elements, terms, ((1536, 128), f32), lanes, ((128, 128), f32), both),
    )
    carried = ()
    for j in range(1, 3):
        send, com, kept, *carried = call(
            functools.partial(next_kernel, j),
            (exchange(send), com, kept, fixed, fac, index, code, *carried),
            (((2048, 128), bf16), matrices, messages, matrices, messages),
            (elements, terms, both),
        )
    recv = exchange(send)
    (send,) = call(
        last_elements,
        (recv, kept, carried[1], fac, index, code),
        (((1024, 128), bf16),),
        (elements, terms, both, messages),
    )
    blocks = call(
        last_matrices,
        (recv, com, carried[0], fixed, send),
        (block, block, block, block),
        (both, matrices),
        any_at=(4,),
    )
    return tuple(
        call(
            sum_kernel,
            (rho_real, rho_imag, to_elements(send, 8), *along_row(*blocks)),
            (part, part),
            (messages, part, part),
        )
    )


def solution(mesh):
    placed = (
        P("aux", "row", None),
        P("aux", "row", None),
        P(),
        P("aux"),
        P("aux", None, None),
        P(),
        P(),
    )
    return jax.shard_map(
        shards,
        mesh=mesh,
        in_specs=placed,
        out_specs=(P("aux", "row", None), P("aux", "row", None)),
        check_vma=False,
    )
```

```python
import functools

import jax
import jax.numpy as jnp
from jax import lax
from jax.experimental import pallas as pl
from jax.experimental.pallas import tpu as pltpu
from jax.sharding import PartitionSpec as P

step_size = 0.1
weights_of = (step_size, step_size**2 / 2.0, step_size**3 / 6.0, step_size**4 / 24.0)
repay = weights_of[0] / weights_of[1]
high = lax.Precision.HIGHEST
f32 = jnp.float32
bf16 = jnp.bfloat16


def swap_blocks(parts):
    chunk = lax.broadcasted_iota(jnp.int32, (32, 128), 1) // 32
    rows = []
    for j in range(4):
        row = None
        for i in range(4):
            shift = (32 * (i - j)) % 128
            moved = parts[i] if shift == 0 else pltpu.roll(parts[i], shift, 1)
            row = moved if row is None else jnp.where(chunk == i, moved, row)
        rows.append(row)
    return rows


def split_rows(block):
    return [block[32 * j : 32 * j + 32] for j in range(4)]


def commutator(state, fixed_ref):
    energy = fixed_ref[0:128, :]
    result = []
    for n in range(4):
        com = []
        for part in range(2):
            x = state[2 * n + part]
            left = jnp.dot(energy, x, precision=high, preferred_element_type=f32)
            right = jnp.dot(x, energy, precision=high, preferred_element_type=f32)
            com.append(left - right)
        rate = fixed_ref[128 + n : 129 + n, :]
        result.append(com[1] - rate * state[2 * n])
        result.append(-com[0] - rate * state[2 * n + 1])
    return result


def load_matrices(rows_ref, first, per_dev, per_row):
    state = [[None] * 4 for _ in range(8)]
    for r in range(4):
        for k in range(2):
            block = rows_ref[pl.ds(per_row * r + first + k, 128, stride=per_dev), :]
            swapped = swap_blocks(split_rows(block))
            for c in range(4):
                state[4 * k + c][r] = swapped[c]
    return [jnp.concatenate(parts, axis=0) for parts in state]


def store_matrices(rows_ref, mats, first, per_dev, per_row):
    for r in range(4):
        for k in range(2):
            parts = [mats[4 * k + c][32 * r : 32 * r + 32, :] for c in range(4)]
            block = jnp.concatenate(swap_blocks(parts), axis=0)
            rows_ref[pl.ds(per_row * r + first + k, 128, stride=per_dev), :] = block


def swap_rows(x):
    lane = lax.broadcasted_iota(jnp.int32, (128, 128), 1)
    row = lax.broadcasted_iota(jnp.int32, (128, 128), 0)
    for s in (1, 2, 4, 8):
        right, low = (lane & (8 * s)) != 0, (row & s) != 0
        ahead = pltpu.roll(pltpu.roll(x, 8 * s, 1), 128 - s, 0)
        behind = pltpu.roll(pltpu.roll(x, 128 - 8 * s, 1), s, 0)
        x = jnp.where(right, jnp.where(low, x, ahead), jnp.where(low, behind, x))
    return x


def load_elements(x_ref, rows_of):
    left = lax.broadcasted_iota(jnp.int32, (64, 128), 1) < 64
    rows = [rows_of(r, k) for r in range(4) for k in range(2)]
    for w in range(0, 16, 2):
        parts = [row[8 * v : 8 * v + 8, :] for v in (w, w + 1) for row in rows]
        turned = jnp.concatenate(parts, axis=0).T
        even, odd = turned[:64], turned[64:]
        x_ref[w] = jnp.where(left, even, pltpu.roll(odd, 64, 1))
        x_ref[w + 1] = jnp.where(left, pltpu.roll(even, 64, 1), odd)


def couple(x_ref, w_ref, fac_ref, index_ref, code_ref, out_ref, exact):
    target = lax.broadcasted_iota(jnp.int32, (256, 128), 0).astype(f32).astype(bf16)
    for g in range(8):
        index = index_ref[16 * g : 16 * g + 16, :]
        code = code_ref[16 * g : 16 * g + 16, :].astype(f32).astype(bf16)
        for w in range(16):
            row = jnp.broadcast_to(index[w : w + 1, :], (8, 128))
            lanes = pl.ds(128 * w, 128)
            for e in range(4):
                at_re, at_im = pl.ds(8 * e, 8), pl.ds(32 + 8 * e, 8)
                x_re = jnp.take_along_axis(x_ref[w, at_re, :], row, axis=1)
                x_im = jnp.take_along_axis(x_ref[w, at_im, :], row, axis=1)
                fac_re, fac_im = fac_ref[16 * g + w, at_re, :], fac_ref[16 * g + w, at_im, :]
                w_ref[g, at_re, lanes] = fac_re * x_re - fac_im * x_im
                w_ref[g, at_im, lanes] = fac_re * x_im + fac_im * x_re
        term = w_ref[g]
        upper = term.astype(bf16)
        marks = jnp.concatenate(
            [jnp.where(target == code[w : w + 1, :], bf16(1), bf16(0)) for w in range(16)], axis=1
        )
        dims = (((1,), (1,)), ((), ()))
        if exact:
            lower = (term - upper.astype(f32)).astype(bf16)
            total = lax.dot_general(marks, jnp.concatenate([upper, lower], axis=0), dims, preferred_element_type=f32)
            total = total[:, :64] + total[:, 64:]
        else:
            total = lax.dot_general(marks, upper, dims, preferred_element_type=f32)
        out_ref[128 * g : 128 * g + 128, :] = jnp.concatenate([total[:128], total[128:]], axis=1)


def rounded_off(x):
    return x - x.astype(bf16).astype(f32)


def pack_kernel(
    re_at, im_at, couplings_at,
    send_ref, own_at, one_at, two_at, three_at,
    rows_ref, re_ref, im_ref, couplings_ref, done,
):
    halves = [pl.ds(0, 8), pl.ds(8, 8)]
    loads = [pltpu.make_async_copy(couplings_at, couplings_ref, done.at[0])]
    for h, half in enumerate(halves):
        loads.append(pltpu.make_async_copy(re_at.at[half], re_ref.at[half], done.at[1 + 2 * h]))
        loads.append(pltpu.make_async_copy(im_at.at[half], im_ref.at[half], done.at[2 + 2 * h]))
    row = lax.axis_index("row")
    blocks = []
    for step, block_at in enumerate((own_at, one_at, two_at, three_at)):
        four = pl.ds(4 * lax.rem(row + step, 4), 4)
        blocks.append(pltpu.make_async_copy(re_ref.at[four], block_at.at[pl.ds(0, 4)], done.at[5 + 2 * step]))
        blocks.append(pltpu.make_async_copy(im_ref.at[four], block_at.at[pl.ds(4, 4)], done.at[6 + 2 * step]))
    for copy in loads:
        copy.start()
    loads[0].wait()
    lane = lax.broadcasted_iota(jnp.int32, (16, 128), 1)
    source = lax.broadcasted_iota(jnp.int32, (16, 128), 0).astype(f32)
    target, mode, weight = (couplings_ref[f].astype(f32).T for f in range(3))
    fields = [jnp.zeros((16, 128), f32) for _ in range(4)]
    for j in range(6):
        to = jnp.broadcast_to(target[:, j : j + 1], (16, 128)).astype(jnp.int32)
        here = (to // 16) == lane
        values = (
            source,
            jnp.broadcast_to(mode[:, j : j + 1], (16, 128)),
            jnp.broadcast_to(weight[:, j : j + 1], (16, 128)),
            (to % 16 + 1).astype(f32),
        )
        fields = [field + jnp.where(here, value, 0.0) for field, value in zip(fields, values)]
    for f in range(4):
        line = jnp.sum(fields[f], axis=0, keepdims=True)
        rows_ref[pl.ds(8 + f, 128, stride=12), :] = jnp.broadcast_to(line, (128, 128))
    for k in range(8):
        if k % 4 == 0:
            loads[1 + k // 2].wait()
            loads[2 + k // 2].wait()
        if k == 4:
            for copy in blocks:
                copy.start()
        parts = [(re_ref, im_ref)[c % 2][2 * k + c // 2] for c in range(4)]
        rows_ref[pl.ds(k, 128, stride=12), :] = jnp.concatenate(swap_blocks(parts), axis=0)
    send_ref[...] = rows_ref[...].astype(bf16)
    for copy in blocks:
        copy.wait()


def first_elements(
    recv_ref, turned_ref, blocks_ref,
    send_ref, fac_ref, index_ref, code_ref, kept_ref,
    x_ref, w_ref, rows_ref, mode_ref, weight_ref, both_ref,
):
    rows_ref[...] = recv_ref[...].astype(f32)
    coded = 0.0
    for f, unit in enumerate((1.0, 16.0, 2048.0, 16384.0)):
        coded = coded + unit * rows_ref[pl.ds(8 + f, 128, stride=12), :]
    coded = swap_rows(coded.T).astype(jnp.int32)
    lane = lax.broadcasted_iota(jnp.int32, (128, 128), 1)
    index_ref[...] = 64 * (coded & 1) + 8 * ((coded >> 1) & 7) + (lane & 7)
    mode_ref[...] = (coded >> 4) & 127
    weight_ref[...] = ((coded >> 11) & 7).astype(f32)
    local = (coded >> 14) - 1
    code_ref[...] = jnp.where(local >= 0, 128 * (local & 1) + (lane & 120) + (local >> 1), -1)

    base = pl.multiple_of(32 * (lax.axis_index("aux") // 32), 32)

    def factors(v, carry):
        at = pl.ds(pl.multiple_of(8 * v, 8), 8)
        modes, weights = mode_ref[at, :], weight_ref[at, :]
        for q in range(8):
            mode = jnp.broadcast_to(modes[q : q + 1, :], (8, 128))
            weight = weights[q : q + 1, :]
            picked = jnp.take_along_axis(turned_ref[128:136, :], mode, axis=1)
            real, imag, own = picked[0:1, :], picked[1:2, :], picked[2:3, :]
            plus = weight * imag
            minus = jnp.where(weight == 0.0, 1.0, weight * real)
            for e in range(4):
                other = jnp.take_along_axis(turned_ref[pl.ds(base + 8 * e, 8), :], mode, axis=1)
                fac_ref[8 * v + q, 8 * e : 8 * e + 8, :] = plus * (own + other)
                fac_ref[8 * v + q, 32 + 8 * e : 40 + 8 * e, :] = -(minus * (own - other))
        return carry

    lax.fori_loop(0, 16, factors, 0, unroll=2)
    load_elements(x_ref, lambda r, k: rows_ref[pl.ds(2 * r + k, 128, stride=12), :])
    couple(x_ref, w_ref, fac_ref, index_ref, code_ref, kept_ref, True)
    for r in range(4):
        for k in range(2):
            both_ref[pl.ds(4 * r + k, 128, stride=16), :] = blocks_ref[2 * r + k]
    send_elements(both_ref, kept_ref)
    send_ref[...] = both_ref[...].astype(bf16)


def send_elements(rows_ref, kept_ref):
    for k in range(8):
        rows_ref[pl.ds(4 * (k // 2) + 2 + k % 2, 128, stride=16), :] = kept_ref[pl.ds(k, 128, stride=8), :]


def first_matrices(
    own_ref, one_ref, two_ref, three_ref, given_ref,
    com_ref, blocks_ref, fixed_ref, turned_ref,
    whole_ref,
):
    d, row = lax.axis_index("aux"), lax.axis_index("row")
    energy = given_ref[0:128, :]
    fixed_ref[0:128, :] = 0.5 * (energy + energy.T)
    lane = lax.broadcasted_iota(jnp.int32, (1, 128), 1)
    for n in range(4):
        rate = jnp.sum(jnp.where(lane == 4 * row + n, given_ref[258:259, :], 0.0), axis=1, keepdims=True)
        fixed_ref[128 + n : 129 + n, :] = jnp.broadcast_to(rate, (1, 128))
    fixed_ref[132:136, :] = jnp.zeros((4, 128), f32)
    turned_ref[0:128, :] = given_ref[128:256, :].T
    turned_ref[128:130, :] = given_ref[256:258, :]
    turned_ref[130:131, :] = turned_ref[pl.ds(32 * row + d % 32, 1), :]
    turned_ref[131:136, :] = jnp.zeros((5, 128), f32)
    for step, block_ref in enumerate((own_ref, one_ref, two_ref, three_ref)):
        at = pl.ds(pl.multiple_of(32 * lax.rem(row - step + 4, 4), 32), 32)
        for m in range(8):
            whole_ref[m, at, :] = block_ref[4 * (m % 2) + m // 2]
    state = [whole_ref[m] for m in range(8)]
    result = commutator(state, fixed_ref)
    for m in range(8):
        com_ref[m] = result[m]
        result[m] = result[m] + repay * rounded_off(state[m])
    for r in range(4):
        for k in range(2):
            parts = [result[4 * k + c][32 * r : 32 * r + 32, :] for c in range(4)]
            blocks_ref[2 * r + k] = jnp.concatenate(swap_blocks(parts), axis=0)


def next_elements(rows_ref, kept_ref, x_ref):
    load_elements(
        x_ref,
        lambda r, k: rows_ref[pl.ds(4 * r + k, 128, stride=16), :] + kept_ref[pl.ds(2 * r + k, 128, stride=8), :],
    )


def next_kernel(
    j, recv_ref, com_ref, kept_ref, fixed_ref, fac_ref, index_ref, code_ref, *rest
):
    if j > 1:
        total_ref, owed_ref, *rest = rest
    send_ref, com_out, kept_out, total_out, owed_out, x_ref, w_ref, rows_ref = rest
    rows_ref[...] = recv_ref[...].astype(f32)
    state = load_matrices(rows_ref, 2, 16, 4)
    state = [state[m] + com_ref[m] for m in range(8)]
    result = commutator(state, fixed_ref)
    for m in range(8):
        total = weights_of[j - 1] * state[m]
        total_out[m] = total + total_ref[m] if j > 1 else total
        com_out[m] = result[m]
    owed = weights_of[j - 1] * rounded_off(kept_ref[...])
    owed_out[...] = owed + owed_ref[...] if j > 1 else owed
    next_elements(rows_ref, kept_ref, x_ref)
    store_matrices(rows_ref, result, 0, 16, 4)
    couple(x_ref, w_ref, fac_ref, index_ref, code_ref, kept_out, False)
    send_elements(rows_ref, kept_out)
    send_ref[...] = rows_ref[...].astype(bf16)


def last_matrices(
    recv_ref, com_ref, total_ref, fixed_ref, after_ref, own_ref, one_ref, two_ref, three_ref, rows_ref, whole_ref
):
    rows_ref[...] = recv_ref[...].astype(f32)
    state = load_matrices(rows_ref, 2, 16, 4)
    state = [state[m] + com_ref[m] for m in range(8)]
    result = commutator(state, fixed_ref)
    for m in range(8):
        total = total_ref[m] + weights_of[2] * state[m] + weights_of[3] * result[m]
        whole_ref[m] = total
    row = lax.axis_index("row")
    for step, block_ref in enumerate((own_ref, one_ref, two_ref, three_ref)):
        at = pl.ds(pl.multiple_of(32 * lax.rem(row + step, 4), 32), 32)
        for m in range(8):
            block_ref[m] = whole_ref[m, at, :]


def last_elements(
    recv_ref, kept_ref, owed_ref, fac_ref, index_ref, code_ref,
    send_ref,
    x_ref, w_ref, rows_ref, out_ref,
):
    rows_ref[...] = recv_ref[...].astype(f32)
    next_elements(rows_ref, kept_ref, x_ref)
    couple(x_ref, w_ref, fac_ref, index_ref, code_ref, out_ref, False)
    owed = owed_ref[...] + weights_of[2] * rounded_off(kept_ref[...])
    send_ref[...] = (weights_of[3] * out_ref[...] + owed).astype(bf16)


def sum_kernel(
    re_ref, im_ref, recv_ref, own_ref, one_ref, two_ref, three_ref, re_out, im_out, rows_ref, re_sum, im_sum
):
    rows_ref[...] = recv_ref[...].astype(f32)
    for k in range(8):
        parts = swap_blocks(split_rows(rows_ref[pl.ds(k, 128, stride=8), :]))
        for c in range(4):
            (re_sum, im_sum)[c % 2][2 * k + c // 2] = parts[c]
    row = lax.axis_index("row")
    for step, block_ref in enumerate((own_ref, one_ref, two_ref, three_ref)):
        first = 4 * lax.rem(row - step + 4, 4)
        for i in range(4):
            n = first + i
            re_out[n] = re_ref[n] + (re_sum[n] + block_ref[2 * i])
            im_out[n] = im_ref[n] + (im_sum[n] + block_ref[2 * i + 1])


def vmem():
    return pl.BlockSpec(memory_space=pltpu.VMEM)


def smem():
    return pl.BlockSpec(memory_space=pltpu.SMEM)


def call(kernel, ins, outs, scratch=(), smem_at=(), any_at=(), any_out=(), room=24):
    return pl.pallas_call(
        kernel,
        out_shape=[jax.ShapeDtypeStruct(shape, dtype) for shape, dtype in outs],
        in_specs=[
            smem() if i in smem_at else pl.BlockSpec(memory_space=pl.ANY) if i in any_at else vmem() for i in range(len(ins))
        ],
        out_specs=[pl.BlockSpec(memory_space=pl.ANY) if i in any_out else vmem() for i in range(len(outs))],
        scratch_shapes=[pltpu.VMEM(*each) if isinstance(each, tuple) else each for each in scratch],
        compiler_params=pltpu.CompilerParams(vmem_limit_bytes=room * 1024 * 1024),
    )(*ins)


lanes = ((128, 128), jnp.int32)
elements = ((16, 64, 128), f32)
terms = ((8, 64, 2048), f32)
matrices = ((8, 128, 128), f32)
messages = ((1024, 128), f32)
both = ((2048, 128), f32)
factors = ((128, 64, 128), f32)
block = ((8, 32, 128), f32)
constants = ((136, 128), f32)
part = ((16, 32, 128), f32)


def shards(rho_real, rho_imag, hamiltonian, damping, couplings, mode_vector, mode_coef):
    def to_elements(x, rows):
        return lax.all_to_all(x.reshape(128 * rows // 4, 4, 128), "aux", 0, 0, tiled=True).reshape(128 * rows, 128)

    def along_row(own, *rest):
        return own, *(
            lax.ppermute(x, "row", [(i, (i + step) % 4) for i in range(4)]) for step, x in enumerate(rest, 1)
        )

    def exchange(x):
        return lax.all_to_all(x.reshape(512, 4, 128), ("aux", "row"), 0, 0, tiled=True).reshape(2048, 128)

    send, *blocks = call(
        pack_kernel,
        (rho_real, rho_imag, jnp.transpose(couplings, (1, 2, 0))),
        (((1536, 128), bf16), block, block, block, block),
        (((1536, 128), f32), part, part, ((3, 6, 16), jnp.int32), pltpu.SemaphoreType.DMA((13,))),
        any_at=(0, 1, 2),
        any_out=(1, 2, 3, 4),
        room=60,
    )
    recv = to_elements(send, 12)
    last_rows = jnp.pad(damping[None], ((0, 5), (0, 112)))
    given = jnp.concatenate([hamiltonian, mode_vector, mode_coef, last_rows], axis=0)
    com, blocks, fixed, turned = call(
        first_matrices,
        (*along_row(*blocks), given),
        (matrices, matrices, constants, constants),
        (matrices,),
    )
    send, fac, index, code, kept = call(
        first_elements,
        (recv, turned, blocks),
        (((2048, 128), bf16), factors, lanes, lanes, messages),
        (elements, terms, ((1536, 128), f32), lanes, ((128, 128), f32), both),
    )
    carried = ()
    for j in range(1, 3):
        send, com, kept, *carried = call(
            functools.partial(next_kernel, j),
            (exchange(send), com, kept, fixed, fac, index, code, *carried),
            (((2048, 128), bf16), matrices, messages, matrices, messages),
            (elements, terms, both),
        )
    recv = exchange(send)
    (send,) = call(
        last_elements,
        (recv, kept, carried[1], fac, index, code),
        (((1024, 128), bf16),),
        (elements, terms, both, messages),
    )
    blocks = call(
        last_matrices,
        (recv, com, carried[0], fixed, send),
        (block, block, block, block),
        (both, matrices),
        any_at=(4,),
    )
    return tuple(
        call(
            sum_kernel,
            (rho_real, rho_imag, to_elements(send, 8), *along_row(*blocks)),
            (part, part),
            (messages, part, part),
        )
    )


def solution(mesh):
    placed = (
        P("aux", "row", None),
        P("aux", "row", None),
        P(),
        P("aux"),
        P("aux", None, None),
        P(),
        P(),
    )
    return jax.shard_map(
        shards,
        mesh=mesh,
        in_specs=placed,
        out_specs=(P("aux", "row", None), P("aux", "row", None)),
        check_vma=False,
    )
```

```python
import functools

import jax
import jax.numpy as jnp
from jax import lax
from jax.experimental import pallas as pl
from jax.experimental.pallas import tpu as pltpu
from jax.sharding import PartitionSpec as P

step_size = 0.1
weights_of = (step_size, step_size**2 / 2.0, step_size**3 / 6.0, step_size**4 / 24.0)
repay = weights_of[0] / weights_of[1]
f32 = jnp.float32
bf16 = jnp.bfloat16


def swap_blocks(parts):
    lane = lax.broadcasted_iota(jnp.int32, (32, 128), 1)
    odd, right = (lane & 32) != 0, (lane & 64) != 0
    one, two, three, four = parts
    one, two = jnp.where(odd, pltpu.roll(two, 32, 1), one), jnp.where(odd, two, pltpu.roll(one, 96, 1))
    three, four = jnp.where(odd, pltpu.roll(four, 32, 1), three), jnp.where(odd, four, pltpu.roll(three, 96, 1))
    one, three = swap_halves(right, one, three)
    two, four = swap_halves(right, two, four)
    return [one, two, three, four]


def swap_halves(right, one, two):
    moved = pltpu.roll(jnp.where(right, one, two), 64, 1)
    return jnp.where(right, moved, one), jnp.where(right, two, moved)


def split_rows(block):
    return [block[32 * j : 32 * j + 32] for j in range(4)]


def in_two(x):
    upper = x.astype(bf16)
    return upper, (x - upper.astype(f32)).astype(bf16)


def product(x, y):
    return jnp.dot(x, y, preferred_element_type=f32)


def commutator(state, fixed_ref):
    upper, lower = in_two(fixed_ref[0:128, :])
    beside, above = jnp.concatenate([upper, upper], axis=1), jnp.concatenate([upper, upper], axis=0)
    result = []
    for n in range(4):
        com = []
        for part in range(2):
            high, low = in_two(state[2 * n + part])
            left = product(beside, jnp.concatenate([high, low], axis=0)) + product(lower, high)
            right = product(jnp.concatenate([high, low], axis=1), above) + product(high, lower)
            com.append(left - right)
        rate = fixed_ref[128 + n : 129 + n, :]
        result.append(com[1] - rate * state[2 * n])
        result.append(-com[0] - rate * state[2 * n + 1])
    return result


def load_matrices(rows_ref, first, per_dev, per_row):
    state = [[None] * 4 for _ in range(8)]
    for r in range(4):
        for k in range(2):
            block = rows_ref[pl.ds(per_row * r + first + k, 128, stride=per_dev), :]
            swapped = swap_blocks(split_rows(block))
            for c in range(4):
                state[4 * k + c][r] = swapped[c]
    return [jnp.concatenate(parts, axis=0) for parts in state]


def store_matrices(rows_ref, mats, first, per_dev, per_row):
    for r in range(4):
        for k in range(2):
            parts = [mats[4 * k + c][32 * r : 32 * r + 32, :] for c in range(4)]
            block = jnp.concatenate(swap_blocks(parts), axis=0)
            rows_ref[pl.ds(per_row * r + first + k, 128, stride=per_dev), :] = block


def swap_rows(x):
    lane = lax.broadcasted_iota(jnp.int32, (128, 128), 1)
    row = lax.broadcasted_iota(jnp.int32, (128, 128), 0)
    for s in (1, 2, 4, 8):
        right, low = (lane & (8 * s)) != 0, (row & s) != 0
        ahead = pltpu.roll(pltpu.roll(x, 8 * s, 1), 128 - s, 0)
        behind = pltpu.roll(pltpu.roll(x, 128 - 8 * s, 1), s, 0)
        x = jnp.where(right, jnp.where(low, x, ahead), jnp.where(low, behind, x))
    return x


def load_elements(x_ref, rows_of):
    right = lax.broadcasted_iota(jnp.int32, (64, 128), 1) >= 64
    rows = [rows_of(r, k) for r in range(4) for k in range(2)]
    for w in range(0, 16, 2):
        parts = [row[8 * v : 8 * v + 8, :] for v in (w, w + 1) for row in rows]
        turned = jnp.concatenate(parts, axis=0).T
        x_ref[w], x_ref[w + 1] = swap_halves(right, turned[:64], turned[64:])


def couple(x_ref, w_ref, fac_ref, index_ref, code_ref, out_ref, exact):
    target = lax.broadcasted_iota(jnp.int32, (256, 128), 0).astype(f32).astype(bf16)
    left = lax.broadcasted_iota(jnp.int32, (128, 128), 1) < 64
    for g in range(8):
        index = index_ref[16 * g : 16 * g + 16, :]
        code = code_ref[16 * g : 16 * g + 16, :].astype(f32).astype(bf16)
        for w in range(16):
            row = jnp.broadcast_to(index[w : w + 1, :], (8, 128))
            lanes = pl.ds(128 * w, 128)
            for e in range(4):
                at_re, at_im = pl.ds(8 * e, 8), pl.ds(32 + 8 * e, 8)
                x_re = jnp.take_along_axis(x_ref[w, at_re, :], row, axis=1)
                x_im = jnp.take_along_axis(x_ref[w, at_im, :], row, axis=1)
                fac_re, fac_im = fac_ref[16 * g + w, at_re, :], fac_ref[16 * g + w, at_im, :]
                w_ref[g, at_re, lanes] = fac_re * x_re - fac_im * x_im
                w_ref[g, at_im, lanes] = fac_re * x_im + fac_im * x_re
        term = w_ref[g]
        upper = term.astype(bf16)
        marks = jnp.concatenate(
            [jnp.where(target == code[w : w + 1, :], bf16(1), bf16(0)) for w in range(16)], axis=1
        )
        dims = (((1,), (1,)), ((), ()))
        if exact:
            lower = (term - upper.astype(f32)).astype(bf16)
            total = lax.dot_general(marks, jnp.concatenate([upper, lower], axis=0), dims, preferred_element_type=f32)
            total = total + pltpu.roll(total, 64, 1)
        else:
            twice = jnp.concatenate([upper, upper], axis=0)
            total = lax.dot_general(marks, twice, dims, preferred_element_type=f32)
        out_ref[128 * g : 128 * g + 128, :] = jnp.where(left, total[:128], total[128:])


def rounded_off(x):
    return x - x.astype(bf16).astype(f32)


def pack_kernel(
    re_at, im_at, couplings_at,
    send_ref,
    rows_ref, re_ref, im_ref, couplings_ref, done,
):
    halves = [pl.ds(0, 8), pl.ds(8, 8)]
    loads = [pltpu.make_async_copy(couplings_at, couplings_ref, done.at[0])]
    for h, half in enumerate(halves):
        loads.append(pltpu.make_async_copy(re_at.at[half], re_ref.at[half], done.at[1 + 2 * h]))
        loads.append(pltpu.make_async_copy(im_at.at[half], im_ref.at[half], done.at[2 + 2 * h]))
    for copy in loads:
        copy.start()
    loads[0].wait()
    lane = lax.broadcasted_iota(jnp.int32, (16, 128), 1)
    source = lax.broadcasted_iota(jnp.int32, (16, 128), 0).astype(f32)
    target, mode, weight = (couplings_ref[f].astype(f32).T for f in range(3))
    fields = [jnp.zeros((16, 128), f32) for _ in range(4)]
    for j in range(6):
        to = jnp.broadcast_to(target[:, j : j + 1], (16, 128)).astype(jnp.int32)
        here = (to // 16) == lane
        values = (
            source,
            jnp.broadcast_to(mode[:, j : j + 1], (16, 128)),
            jnp.broadcast_to(weight[:, j : j + 1], (16, 128)),
            (to % 16 + 1).astype(f32),
        )
        fields = [field + jnp.where(here, value, 0.0) for field, value in zip(fields, values)]
    for f in range(4):
        line = jnp.sum(fields[f], axis=0, keepdims=True)
        rows_ref[pl.ds(8 + f, 128, stride=12), :] = jnp.broadcast_to(line, (128, 128))
    for k in range(8):
        if k % 4 == 0:
            loads[1 + k // 2].wait()
            loads[2 + k // 2].wait()
        parts = [(re_ref, im_ref)[c % 2][2 * k + c // 2] for c in range(4)]
        rows_ref[pl.ds(k, 128, stride=12), :] = jnp.concatenate(swap_blocks(parts), axis=0)
    send_ref[...] = rows_ref[...].astype(bf16)


def block_kernel(re_at, im_at, after_ref, own_ref, one_ref, two_ref, three_ref, done):
    row = lax.axis_index("row")
    copies = []
    for step, block_ref in enumerate((own_ref, one_ref, two_ref, three_ref)):
        four = pl.ds(4 * lax.rem(row + step, 4), 4)
        copies.append(pltpu.make_async_copy(re_at.at[four], block_ref.at[pl.ds(0, 4)], done.at[2 * step]))
        copies.append(pltpu.make_async_copy(im_at.at[four], block_ref.at[pl.ds(4, 4)], done.at[2 * step + 1]))
    for copy in copies:
        copy.start()
    for copy in copies:
        copy.wait()


def first_elements(
    recv_ref, turned_ref, blocks_ref,
    send_ref, fac_ref, index_ref, code_ref, kept_ref,
    x_ref, w_ref, rows_ref, mode_ref, weight_ref, both_ref,
):
    rows_ref[...] = recv_ref[...].astype(f32)
    coded = 0.0
    for f, unit in enumerate((1.0, 16.0, 2048.0, 16384.0)):
        coded = coded + unit * rows_ref[pl.ds(8 + f, 128, stride=12), :]
    coded = swap_rows(coded.T).astype(jnp.int32)
    lane = lax.broadcasted_iota(jnp.int32, (128, 128), 1)
    index_ref[...] = 64 * (coded & 1) + 8 * ((coded >> 1) & 7) + (lane & 7)
    mode_ref[...] = (coded >> 4) & 127
    weight_ref[...] = ((coded >> 11) & 7).astype(f32)
    local = (coded >> 14) - 1
    code_ref[...] = jnp.where(local >= 0, 128 * (local & 1) + (lane & 120) + (local >> 1), -1)

    base = pl.multiple_of(32 * (lax.axis_index("aux") // 32), 32)

    def factors(v, carry):
        at = pl.ds(pl.multiple_of(8 * v, 8), 8)
        modes, weights = mode_ref[at, :], weight_ref[at, :]
        for q in range(8):
            mode = jnp.broadcast_to(modes[q : q + 1, :], (8, 128))
            weight = weights[q : q + 1, :]
            picked = jnp.take_along_axis(turned_ref[128:136, :], mode, axis=1)
            real, imag, own = picked[0:1, :], picked[1:2, :], picked[2:3, :]
            plus = weight * imag
            minus = jnp.where(weight == 0.0, 1.0, weight * real)
            for e in range(4):
                other = jnp.take_along_axis(turned_ref[pl.ds(base + 8 * e, 8), :], mode, axis=1)
                fac_ref[8 * v + q, 8 * e : 8 * e + 8, :] = plus * (own + other)
                fac_ref[8 * v + q, 32 + 8 * e : 40 + 8 * e, :] = -(minus * (own - other))
        return carry

    lax.fori_loop(0, 16, factors, 0, unroll=2)
    load_elements(x_ref, lambda r, k: rows_ref[pl.ds(2 * r + k, 128, stride=12), :])
    couple(x_ref, w_ref, fac_ref, index_ref, code_ref, kept_ref, True)
    for r in range(4):
        for k in range(2):
            both_ref[pl.ds(4 * r + k, 128, stride=16), :] = blocks_ref[2 * r + k]
    send_elements(both_ref, kept_ref)
    send_ref[...] = both_ref[...].astype(bf16)


def send_elements(rows_ref, kept_ref):
    for k in range(8):
        rows_ref[pl.ds(4 * (k // 2) + 2 + k % 2, 128, stride=16), :] = kept_ref[pl.ds(k, 128, stride=8), :]


def first_matrices(
    own_ref, one_ref, two_ref, three_ref, given_ref,
    com_ref, blocks_ref, fixed_ref, turned_ref,
    whole_ref,
):
    d, row = lax.axis_index("aux"), lax.axis_index("row")
    energy = given_ref[0:128, :]
    fixed_ref[0:128, :] = 0.5 * (energy + energy.T)
    lane = lax.broadcasted_iota(jnp.int32, (1, 128), 1)
    for n in range(4):
        rate = jnp.sum(jnp.where(lane == 4 * row + n, given_ref[258:259, :], 0.0), axis=1, keepdims=True)
        fixed_ref[128 + n : 129 + n, :] = jnp.broadcast_to(rate, (1, 128))
    fixed_ref[132:136, :] = jnp.zeros((4, 128), f32)
    turned_ref[0:128, :] = given_ref[128:256, :].T
    turned_ref[128:130, :] = given_ref[256:258, :]
    turned_ref[130:131, :] = turned_ref[pl.ds(32 * row + d % 32, 1), :]
    turned_ref[131:136, :] = jnp.zeros((5, 128), f32)
    for step, block_ref in enumerate((own_ref, one_ref, two_ref, three_ref)):
        at = pl.ds(pl.multiple_of(32 * lax.rem(row - step + 4, 4), 32), 32)
        for m in range(8):
            whole_ref[m, at, :] = block_ref[4 * (m % 2) + m // 2]
    state = [whole_ref[m] for m in range(8)]
    result = commutator(state, fixed_ref)
    for m in range(8):
        com_ref[m] = result[m]
        result[m] = result[m] + repay * rounded_off(state[m])
    for r in range(4):
        for k in range(2):
            parts = [result[4 * k + c][32 * r : 32 * r + 32, :] for c in range(4)]
            blocks_ref[2 * r + k] = jnp.concatenate(swap_blocks(parts), axis=0)


def next_elements(rows_ref, kept_ref, x_ref):
    load_elements(
        x_ref,
        lambda r, k: rows_ref[pl.ds(4 * r + k, 128, stride=16), :] + kept_ref[pl.ds(2 * r + k, 128, stride=8), :],
    )


def next_kernel(
    j, recv_ref, com_ref, kept_ref, fixed_ref, fac_ref, index_ref, code_ref, *rest
):
    if j > 1:
        total_ref, owed_ref, *rest = rest
    send_ref, com_out, kept_out, total_out, owed_out, x_ref, w_ref, rows_ref = rest
    rows_ref[...] = recv_ref[...].astype(f32)
    state = load_matrices(rows_ref, 2, 16, 4)
    state = [state[m] + com_ref[m] for m in range(8)]
    result = commutator(state, fixed_ref)
    for m in range(8):
        total = weights_of[j - 1] * state[m]
        total_out[m] = total + total_ref[m] if j > 1 else total
        com_out[m] = result[m]
    owed = weights_of[j - 1] * rounded_off(kept_ref[...])
    owed_out[...] = owed + owed_ref[...] if j > 1 else owed
    next_elements(rows_ref, kept_ref, x_ref)
    store_matrices(rows_ref, result, 0, 16, 4)
    couple(x_ref, w_ref, fac_ref, index_ref, code_ref, kept_out, False)
    send_elements(rows_ref, kept_out)
    send_ref[...] = rows_ref[...].astype(bf16)


def last_matrices(
    recv_ref, com_ref, total_ref, fixed_ref, after_ref, own_ref, one_ref, two_ref, three_ref, rows_ref, whole_ref
):
    rows_ref[...] = recv_ref[...].astype(f32)
    state = load_matrices(rows_ref, 2, 16, 4)
    state = [state[m] + com_ref[m] for m in range(8)]
    result = commutator(state, fixed_ref)
    for m in range(8):
        total = total_ref[m] + weights_of[2] * state[m] + weights_of[3] * result[m]
        whole_ref[m] = total
    row = lax.axis_index("row")
    for step, block_ref in enumerate((own_ref, one_ref, two_ref, three_ref)):
        at = pl.ds(pl.multiple_of(32 * lax.rem(row + step, 4), 32), 32)
        for m in range(8):
            block_ref[m] = whole_ref[m, at, :]


def last_elements(
    recv_ref, kept_ref, owed_ref, fac_ref, index_ref, code_ref,
    send_ref,
    x_ref, w_ref, rows_ref, out_ref,
):
    rows_ref[...] = recv_ref[...].astype(f32)
    next_elements(rows_ref, kept_ref, x_ref)
    couple(x_ref, w_ref, fac_ref, index_ref, code_ref, out_ref, False)
    owed = owed_ref[...] + weights_of[2] * rounded_off(kept_ref[...])
    send_ref[...] = (weights_of[3] * out_ref[...] + owed).astype(bf16)


def sum_kernel(
    re_ref, im_ref, recv_ref, own_ref, one_ref, two_ref, three_ref, re_out, im_out, rows_ref, re_sum, im_sum
):
    rows_ref[...] = recv_ref[...].astype(f32)
    for k in range(8):
        parts = swap_blocks(split_rows(rows_ref[pl.ds(k, 128, stride=8), :]))
        for c in range(4):
            (re_sum, im_sum)[c % 2][2 * k + c // 2] = parts[c]
    row = lax.axis_index("row")
    for step, block_ref in enumerate((own_ref, one_ref, two_ref, three_ref)):
        first = 4 * lax.rem(row - step + 4, 4)
        for i in range(4):
            n = first + i
            re_out[n] = re_ref[n] + (re_sum[n] + block_ref[2 * i])
            im_out[n] = im_ref[n] + (im_sum[n] + block_ref[2 * i + 1])


def vmem():
    return pl.BlockSpec(memory_space=pltpu.VMEM)


def smem():
    return pl.BlockSpec(memory_space=pltpu.SMEM)


def call(kernel, ins, outs, scratch=(), smem_at=(), any_at=(), room=24):
    return pl.pallas_call(
        kernel,
        out_shape=[jax.ShapeDtypeStruct(shape, dtype) for shape, dtype in outs],
        in_specs=[
            smem() if i in smem_at else pl.BlockSpec(memory_space=pl.ANY) if i in any_at else vmem() for i in range(len(ins))
        ],
        out_specs=[vmem() for _ in outs],
        scratch_shapes=[pltpu.VMEM(*each) if isinstance(each, tuple) else each for each in scratch],
        compiler_params=pltpu.CompilerParams(vmem_limit_bytes=room * 1024 * 1024),
    )(*ins)


lanes = ((128, 128), jnp.int32)
elements = ((16, 64, 128), f32)
terms = ((8, 64, 2048), f32)
matrices = ((8, 128, 128), f32)
messages = ((1024, 128), f32)
both = ((2048, 128), f32)
factors = ((128, 64, 128), f32)
block = ((8, 32, 128), f32)
constants = ((136, 128), f32)
part = ((16, 32, 128), f32)


def shards(rho_real, rho_imag, hamiltonian, damping, couplings, mode_vector, mode_coef):
    def to_elements(x, rows):
        return lax.all_to_all(x.reshape(128 * rows // 4, 4, 128), "aux", 0, 0, tiled=True).reshape(128 * rows, 128)

    def along_row(own, *rest):
        return own, *(
            lax.ppermute(x, "row", [(i, (i + step) % 4) for i in range(4)]) for step, x in enumerate(rest, 1)
        )

    def exchange(x):
        return lax.all_to_all(x.reshape(512, 4, 128), ("aux", "row"), 0, 0, tiled=True).reshape(2048, 128)

    (send,) = call(
        pack_kernel,
        (rho_real, rho_imag, jnp.transpose(couplings, (1, 2, 0))),
        (((1536, 128), bf16),),
        (((1536, 128), f32), part, part, ((3, 6, 16), jnp.int32), pltpu.SemaphoreType.DMA((5,))),
        any_at=(0, 1, 2),
        room=60,
    )
    recv = to_elements(send, 12)
    blocks = call(
        block_kernel,
        (rho_real, rho_imag, send),
        (block, block, block, block),
        (pltpu.SemaphoreType.DMA((8,)),),
        any_at=(0, 1, 2),
        room=60,
    )
    last_rows = jnp.pad(damping[None], ((0, 5), (0, 112)))
    given = jnp.concatenate([hamiltonian, mode_vector, mode_coef, last_rows], axis=0)
    com, blocks, fixed, turned = call(
        first_matrices,
        (*along_row(*blocks), given),
        (matrices, matrices, constants, constants),
        (matrices,),
    )
    send, fac, index, code, kept = call(
        first_elements,
        (recv, turned, blocks),
        (((2048, 128), bf16), factors, lanes, lanes, messages),
        (elements, terms, ((1536, 128), f32), lanes, ((128, 128), f32), both),
    )
    carried = ()
    for j in range(1, 3):
        send, com, kept, *carried = call(
            functools.partial(next_kernel, j),
            (exchange(send), com, kept, fixed, fac, index, code, *carried),
            (((2048, 128), bf16), matrices, messages, matrices, messages),
            (elements, terms, both),
        )
    recv = exchange(send)
    (send,) = call(
        last_elements,
        (recv, kept, carried[1], fac, index, code),
        (((1024, 128), bf16),),
        (elements, terms, both, messages),
    )
    blocks = call(
        last_matrices,
        (recv, com, carried[0], fixed, send),
        (block, block, block, block),
        (both, matrices),
        any_at=(4,),
    )
    return tuple(
        call(
            sum_kernel,
            (rho_real, rho_imag, to_elements(send, 8), *along_row(*blocks)),
            (part, part),
            (messages, part, part),
        )
    )


def solution(mesh):
    placed = (
        P("aux", "row", None),
        P("aux", "row", None),
        P(),
        P("aux"),
        P("aux", None, None),
        P(),
        P(),
    )
    return jax.shard_map(
        shards,
        mesh=mesh,
        in_specs=placed,
        out_specs=(P("aux", "row", None), P("aux", "row", None)),
        check_vma=False,
    )
```

```python
import functools

import jax
import jax.numpy as jnp
from jax import lax
from jax.experimental import pallas as pl
from jax.experimental.pallas import tpu as pltpu
from jax.sharding import PartitionSpec as P

step_size = 0.1
weights_of = (step_size, step_size**2 / 2.0, step_size**3 / 6.0, step_size**4 / 24.0)
repay = weights_of[0] / weights_of[1]
f32 = jnp.float32
bf16 = jnp.bfloat16


def swap_blocks(parts):
    lane = lax.broadcasted_iota(jnp.int32, (32, 128), 1)
    odd, right = (lane & 32) != 0, (lane & 64) != 0
    one, two, three, four = parts
    one, two = jnp.where(odd, pltpu.roll(two, 32, 1), one), jnp.where(odd, two, pltpu.roll(one, 96, 1))
    three, four = jnp.where(odd, pltpu.roll(four, 32, 1), three), jnp.where(odd, four, pltpu.roll(three, 96, 1))
    one, three = swap_halves(right, one, three)
    two, four = swap_halves(right, two, four)
    return [one, two, three, four]


def swap_halves(right, one, two):
    moved = pltpu.roll(jnp.where(right, one, two), 64, 1)
    return jnp.where(right, moved, one), jnp.where(right, two, moved)


def split_rows(block):
    return [block[32 * j : 32 * j + 32] for j in range(4)]


def in_two(x):
    upper = x.astype(bf16)
    return upper, (x - upper.astype(f32)).astype(bf16)


def product(x, y):
    return jnp.dot(x, y, preferred_element_type=f32)


def commutator(state, fixed_ref):
    upper, lower = in_two(fixed_ref[0:128, :])
    beside, above = jnp.concatenate([upper, upper], axis=1), jnp.concatenate([upper, upper], axis=0)
    result = []
    for n in range(4):
        com = []
        for part in range(2):
            high, low = in_two(state[2 * n + part])
            left = product(beside, jnp.concatenate([high, low], axis=0)) + product(lower, high)
            right = product(jnp.concatenate([high, low], axis=1), above) + product(high, lower)
            com.append(left - right)
        rate = fixed_ref[128 + n : 129 + n, :]
        result.append(com[1] - rate * state[2 * n])
        result.append(-com[0] - rate * state[2 * n + 1])
    return result


def load_matrices(rows_ref, first, per_dev, per_row):
    state = [[None] * 4 for _ in range(8)]
    for r in range(4):
        for k in range(2):
            block = rows_ref[pl.ds(per_row * r + first + k, 128, stride=per_dev), :]
            swapped = swap_blocks(split_rows(block))
            for c in range(4):
                state[4 * k + c][r] = swapped[c]
    return [jnp.concatenate(parts, axis=0) for parts in state]


def store_matrices(rows_ref, mats, first, per_dev, per_row):
    for r in range(4):
        for k in range(2):
            parts = [mats[4 * k + c][32 * r : 32 * r + 32, :] for c in range(4)]
            block = jnp.concatenate(swap_blocks(parts), axis=0)
            rows_ref[pl.ds(per_row * r + first + k, 128, stride=per_dev), :] = block


def swap_rows(x):
    lane = lax.broadcasted_iota(jnp.int32, (128, 128), 1)
    row = lax.broadcasted_iota(jnp.int32, (128, 128), 0)
    for s in (1, 2, 4, 8):
        right, low = (lane & (8 * s)) != 0, (row & s) != 0
        ahead = pltpu.roll(pltpu.roll(x, 8 * s, 1), 128 - s, 0)
        behind = pltpu.roll(pltpu.roll(x, 128 - 8 * s, 1), s, 0)
        x = jnp.where(right, jnp.where(low, x, ahead), jnp.where(low, behind, x))
    return x


def load_elements(x_ref, rows_of):
    right = lax.broadcasted_iota(jnp.int32, (64, 128), 1) >= 64
    rows = [rows_of(r, k) for r in range(4) for k in range(2)]
    for w in range(0, 16, 2):
        parts = [row[8 * v : 8 * v + 8, :] for v in (w, w + 1) for row in rows]
        turned = jnp.concatenate(parts, axis=0).T
        x_ref[w], x_ref[w + 1] = swap_halves(right, turned[:64], turned[64:])


def couple(x_ref, w_ref, fac_ref, index_ref, code_ref, out_ref, exact):
    target = lax.broadcasted_iota(jnp.int32, (256, 128), 0).astype(f32).astype(bf16)
    left = lax.broadcasted_iota(jnp.int32, (128, 128), 1) < 64
    dims = (((1,), (1,)), ((), ()))

    def gather(g, first):
        for w in range(first, first + 8):
            row = jnp.broadcast_to(index_ref[16 * g + w : 16 * g + w + 1, :], (8, 128))
            lanes = pl.ds(128 * w, 128)
            for e in range(4):
                at_re, at_im = pl.ds(8 * e, 8), pl.ds(32 + 8 * e, 8)
                x_re = jnp.take_along_axis(x_ref[w, at_re, :], row, axis=1)
                x_im = jnp.take_along_axis(x_ref[w, at_im, :], row, axis=1)
                fac_re, fac_im = fac_ref[16 * g + w, at_re, :], fac_ref[16 * g + w, at_im, :]
                w_ref[g, at_re, lanes] = fac_re * x_re - fac_im * x_im
                w_ref[g, at_im, lanes] = fac_re * x_im + fac_im * x_re

    def add_up(g, first):
        code = code_ref[16 * g : 16 * g + 16, :].astype(f32).astype(bf16)
        term = w_ref[g, :, 128 * first : 128 * first + 1024]
        upper = term.astype(bf16)
        other = (term - upper.astype(f32)).astype(bf16) if exact else upper
        marks = jnp.concatenate(
            [jnp.where(target == code[w : w + 1, :], bf16(1), bf16(0)) for w in range(first, first + 8)], axis=1
        )
        return lax.dot_general(marks, jnp.concatenate([upper, other], axis=0), dims, preferred_element_type=f32)

    steps = [(g, first) for g in range(8) for first in (0, 8)]
    gather(*steps[0])
    for at, (g, first) in enumerate(steps):
        if at + 1 < len(steps):
            gather(*steps[at + 1])
        part = add_up(g, first)
        total = part if first == 0 else total + part
        if first == 8:
            if exact:
                total = total + pltpu.roll(total, 64, 1)
            out_ref[128 * g : 128 * g + 128, :] = jnp.where(left, total[:128], total[128:])


def rounded_off(x):
    return x - x.astype(bf16).astype(f32)


def pack_kernel(
    re_at, im_at, couplings_at,
    send_ref,
    rows_ref, re_ref, im_ref, couplings_ref, done,
):
    halves = [pl.ds(0, 8), pl.ds(8, 8)]
    loads = [pltpu.make_async_copy(couplings_at, couplings_ref, done.at[0])]
    for h, half in enumerate(halves):
        loads.append(pltpu.make_async_copy(re_at.at[half], re_ref.at[half], done.at[1 + 2 * h]))
        loads.append(pltpu.make_async_copy(im_at.at[half], im_ref.at[half], done.at[2 + 2 * h]))
    for copy in loads:
        copy.start()
    loads[0].wait()
    lane = lax.broadcasted_iota(jnp.int32, (16, 128), 1)
    source = lax.broadcasted_iota(jnp.int32, (16, 128), 0).astype(f32)
    target, mode, weight = (couplings_ref[f].astype(f32).T for f in range(3))
    fields = [jnp.zeros((16, 128), f32) for _ in range(4)]
    for j in range(6):
        to = jnp.broadcast_to(target[:, j : j + 1], (16, 128)).astype(jnp.int32)
        here = (to // 16) == lane
        values = (
            source,
            jnp.broadcast_to(mode[:, j : j + 1], (16, 128)),
            jnp.broadcast_to(weight[:, j : j + 1], (16, 128)),
            (to % 16 + 1).astype(f32),
        )
        fields = [field + jnp.where(here, value, 0.0) for field, value in zip(fields, values)]
    for f in range(4):
        line = jnp.sum(fields[f], axis=0, keepdims=True)
        rows_ref[pl.ds(8 + f, 128, stride=12), :] = jnp.broadcast_to(line, (128, 128))
    for k in range(8):
        if k % 4 == 0:
            loads[1 + k // 2].wait()
            loads[2 + k // 2].wait()
        parts = [(re_ref, im_ref)[c % 2][2 * k + c // 2] for c in range(4)]
        rows_ref[pl.ds(k, 128, stride=12), :] = jnp.concatenate(swap_blocks(parts), axis=0)
    send_ref[...] = rows_ref[...].astype(bf16)


def block_kernel(re_at, im_at, after_ref, own_ref, one_ref, two_ref, three_ref, done):
    row = lax.axis_index("row")
    copies = []
    for step, block_ref in enumerate((own_ref, one_ref, two_ref, three_ref)):
        four = pl.ds(4 * lax.rem(row + step, 4), 4)
        copies.append(pltpu.make_async_copy(re_at.at[four], block_ref.at[pl.ds(0, 4)], done.at[2 * step]))
        copies.append(pltpu.make_async_copy(im_at.at[four], block_ref.at[pl.ds(4, 4)], done.at[2 * step + 1]))
    for copy in copies:
        copy.start()
    for copy in copies:
        copy.wait()


def first_elements(
    recv_ref, turned_ref, blocks_ref,
    send_ref, fac_ref, index_ref, code_ref, kept_ref,
    x_ref, w_ref, rows_ref, mode_ref, weight_ref, both_ref,
):
    rows_ref[...] = recv_ref[...].astype(f32)
    coded = 0.0
    for f, unit in enumerate((1.0, 16.0, 2048.0, 16384.0)):
        coded = coded + unit * rows_ref[pl.ds(8 + f, 128, stride=12), :]
    coded = swap_rows(coded.T).astype(jnp.int32)
    lane = lax.broadcasted_iota(jnp.int32, (128, 128), 1)
    index_ref[...] = 64 * (coded & 1) + 8 * ((coded >> 1) & 7) + (lane & 7)
    mode_ref[...] = (coded >> 4) & 127
    weight_ref[...] = ((coded >> 11) & 7).astype(f32)
    local = (coded >> 14) - 1
    code_ref[...] = jnp.where(local >= 0, 128 * (local & 1) + (lane & 120) + (local >> 1), -1)

    base = pl.multiple_of(32 * (lax.axis_index("aux") // 32), 32)

    def factors(v, carry):
        at = pl.ds(pl.multiple_of(8 * v, 8), 8)
        modes, weights = mode_ref[at, :], weight_ref[at, :]
        for q in range(8):
            mode = jnp.broadcast_to(modes[q : q + 1, :], (8, 128))
            weight = weights[q : q + 1, :]
            picked = jnp.take_along_axis(turned_ref[128:136, :], mode, axis=1)
            real, imag, own = picked[0:1, :], picked[1:2, :], picked[2:3, :]
            plus = weight * imag
            minus = jnp.where(weight == 0.0, 1.0, weight * real)
            for e in range(4):
                other = jnp.take_along_axis(turned_ref[pl.ds(base + 8 * e, 8), :], mode, axis=1)
                fac_ref[8 * v + q, 8 * e : 8 * e + 8, :] = plus * (own + other)
                fac_ref[8 * v + q, 32 + 8 * e : 40 + 8 * e, :] = -(minus * (own - other))
        return carry

    lax.fori_loop(0, 16, factors, 0, unroll=2)
    load_elements(x_ref, lambda r, k: rows_ref[pl.ds(2 * r + k, 128, stride=12), :])
    couple(x_ref, w_ref, fac_ref, index_ref, code_ref, kept_ref, True)
    for r in range(4):
        for k in range(2):
            both_ref[pl.ds(4 * r + k, 128, stride=16), :] = blocks_ref[2 * r + k]
    send_elements(both_ref, kept_ref)
    send_ref[...] = both_ref[...].astype(bf16)


def send_elements(rows_ref, kept_ref):
    for k in range(8):
        rows_ref[pl.ds(4 * (k // 2) + 2 + k % 2, 128, stride=16), :] = kept_ref[pl.ds(k, 128, stride=8), :]


def first_matrices(
    own_ref, one_ref, two_ref, three_ref, given_ref,
    com_ref, blocks_ref, fixed_ref, turned_ref,
    whole_ref,
):
    d, row = lax.axis_index("aux"), lax.axis_index("row")
    energy = given_ref[0:128, :]
    fixed_ref[0:128, :] = 0.5 * (energy + energy.T)
    lane = lax.broadcasted_iota(jnp.int32, (1, 128), 1)
    for n in range(4):
        rate = jnp.sum(jnp.where(lane == 4 * row + n, given_ref[258:259, :], 0.0), axis=1, keepdims=True)
        fixed_ref[128 + n : 129 + n, :] = jnp.broadcast_to(rate, (1, 128))
    fixed_ref[132:136, :] = jnp.zeros((4, 128), f32)
    turned_ref[0:128, :] = given_ref[128:256, :].T
    turned_ref[128:130, :] = given_ref[256:258, :]
    turned_ref[130:131, :] = turned_ref[pl.ds(32 * row + d % 32, 1), :]
    turned_ref[131:136, :] = jnp.zeros((5, 128), f32)
    for step, block_ref in enumerate((own_ref, one_ref, two_ref, three_ref)):
        at = pl.ds(pl.multiple_of(32 * lax.rem(row - step + 4, 4), 32), 32)
        for m in range(8):
            whole_ref[m, at, :] = block_ref[4 * (m % 2) + m // 2]
    state = [whole_ref[m] for m in range(8)]
    result = commutator(state, fixed_ref)
    for m in range(8):
        com_ref[m] = result[m]
        result[m] = result[m] + repay * rounded_off(state[m])
    for r in range(4):
        for k in range(2):
            parts = [result[4 * k + c][32 * r : 32 * r + 32, :] for c in range(4)]
            blocks_ref[2 * r + k] = jnp.concatenate(swap_blocks(parts), axis=0)


def next_elements(rows_ref, kept_ref, x_ref):
    load_elements(
        x_ref,
        lambda r, k: rows_ref[pl.ds(4 * r + k, 128, stride=16), :] + kept_ref[pl.ds(2 * r + k, 128, stride=8), :],
    )


def next_kernel(
    j, recv_ref, com_ref, kept_ref, fixed_ref, fac_ref, index_ref, code_ref, *rest
):
    if j > 1:
        total_ref, owed_ref, *rest = rest
    send_ref, com_out, kept_out, total_out, owed_out, x_ref, w_ref, rows_ref = rest
    rows_ref[...] = recv_ref[...].astype(f32)
    state = load_matrices(rows_ref, 2, 16, 4)
    state = [state[m] + com_ref[m] for m in range(8)]
    result = commutator(state, fixed_ref)
    for m in range(8):
        total = weights_of[j - 1] * state[m]
        total_out[m] = total + total_ref[m] if j > 1 else total
        com_out[m] = result[m]
    owed = weights_of[j - 1] * rounded_off(kept_ref[...])
    owed_out[...] = owed + owed_ref[...] if j > 1 else owed
    next_elements(rows_ref, kept_ref, x_ref)
    store_matrices(rows_ref, result, 0, 16, 4)
    couple(x_ref, w_ref, fac_ref, index_ref, code_ref, kept_out, False)
    send_elements(rows_ref, kept_out)
    send_ref[...] = rows_ref[...].astype(bf16)


def last_matrices(
    recv_ref, com_ref, total_ref, fixed_ref, after_ref, own_ref, one_ref, two_ref, three_ref, rows_ref, whole_ref
):
    rows_ref[...] = recv_ref[...].astype(f32)
    state = load_matrices(rows_ref, 2, 16, 4)
    state = [state[m] + com_ref[m] for m in range(8)]
    result = commutator(state, fixed_ref)
    for m in range(8):
        total = total_ref[m] + weights_of[2] * state[m] + weights_of[3] * result[m]
        whole_ref[m] = total
    row = lax.axis_index("row")
    for step, block_ref in enumerate((own_ref, one_ref, two_ref, three_ref)):
        at = pl.ds(pl.multiple_of(32 * lax.rem(row + step, 4), 32), 32)
        for m in range(8):
            block_ref[m] = whole_ref[m, at, :]


def last_elements(
    recv_ref, kept_ref, owed_ref, fac_ref, index_ref, code_ref,
    send_ref,
    x_ref, w_ref, rows_ref, out_ref,
):
    rows_ref[...] = recv_ref[...].astype(f32)
    next_elements(rows_ref, kept_ref, x_ref)
    couple(x_ref, w_ref, fac_ref, index_ref, code_ref, out_ref, False)
    owed = owed_ref[...] + weights_of[2] * rounded_off(kept_ref[...])
    send_ref[...] = (weights_of[3] * out_ref[...] + owed).astype(bf16)


def base_kernel(re_ref, im_ref, own_ref, one_ref, two_ref, three_ref, re_out, im_out):
    row = lax.axis_index("row")
    for step, block_ref in enumerate((own_ref, one_ref, two_ref, three_ref)):
        first = 4 * lax.rem(row - step + 4, 4)
        for i in range(4):
            re_out[first + i] = re_ref[first + i] + block_ref[2 * i]
            im_out[first + i] = im_ref[first + i] + block_ref[2 * i + 1]


def sum_kernel(re_ref, im_ref, recv_ref, re_out, im_out, rows_ref):
    rows_ref[...] = recv_ref[...].astype(f32)
    for k in range(8):
        parts = swap_blocks(split_rows(rows_ref[pl.ds(k, 128, stride=8), :]))
        for c in range(4):
            source, result = ((re_ref, re_out), (im_ref, im_out))[c % 2]
            n = 2 * k + c // 2
            result[n] = source[n] + parts[c]


def vmem():
    return pl.BlockSpec(memory_space=pltpu.VMEM)


def smem():
    return pl.BlockSpec(memory_space=pltpu.SMEM)


def call(kernel, ins, outs, scratch=(), smem_at=(), any_at=(), room=24):
    return pl.pallas_call(
        kernel,
        out_shape=[jax.ShapeDtypeStruct(shape, dtype) for shape, dtype in outs],
        in_specs=[
            smem() if i in smem_at else pl.BlockSpec(memory_space=pl.ANY) if i in any_at else vmem() for i in range(len(ins))
        ],
        out_specs=[vmem() for _ in outs],
        scratch_shapes=[pltpu.VMEM(*each) if isinstance(each, tuple) else each for each in scratch],
        compiler_params=pltpu.CompilerParams(vmem_limit_bytes=room * 1024 * 1024),
    )(*ins)


lanes = ((128, 128), jnp.int32)
elements = ((16, 64, 128), f32)
terms = ((8, 64, 2048), f32)
matrices = ((8, 128, 128), f32)
messages = ((1024, 128), f32)
both = ((2048, 128), f32)
factors = ((128, 64, 128), f32)
block = ((8, 32, 128), f32)
constants = ((136, 128), f32)
part = ((16, 32, 128), f32)


def shards(rho_real, rho_imag, hamiltonian, damping, couplings, mode_vector, mode_coef):
    def to_elements(x, rows):
        return lax.all_to_all(x.reshape(128 * rows // 4, 4, 128), "aux", 0, 0, tiled=True).reshape(128 * rows, 128)

    def along_row(own, *rest):
        return own, *(
            lax.ppermute(x, "row", [(i, (i + step) % 4) for i in range(4)]) for step, x in enumerate(rest, 1)
        )

    def exchange(x):
        return lax.all_to_all(x.reshape(512, 4, 128), ("aux", "row"), 0, 0, tiled=True).reshape(2048, 128)

    (send,) = call(
        pack_kernel,
        (rho_real, rho_imag, jnp.transpose(couplings, (1, 2, 0))),
        (((1536, 128), bf16),),
        (((1536, 128), f32), part, part, ((3, 6, 16), jnp.int32), pltpu.SemaphoreType.DMA((5,))),
        any_at=(0, 1, 2),
        room=60,
    )
    recv = to_elements(send, 12)
    blocks = call(
        block_kernel,
        (rho_real, rho_imag, send),
        (block, block, block, block),
        (pltpu.SemaphoreType.DMA((8,)),),
        any_at=(0, 1, 2),
        room=60,
    )
    last_rows = jnp.pad(damping[None], ((0, 5), (0, 112)))
    given = jnp.concatenate([hamiltonian, mode_vector, mode_coef, last_rows], axis=0)
    com, blocks, fixed, turned = call(
        first_matrices,
        (*along_row(*blocks), given),
        (matrices, matrices, constants, constants),
        (matrices,),
    )
    send, fac, index, code, kept = call(
        first_elements,
        (recv, turned, blocks),
        (((2048, 128), bf16), factors, lanes, lanes, messages),
        (elements, terms, ((1536, 128), f32), lanes, ((128, 128), f32), both),
    )
    carried = ()
    for j in range(1, 3):
        send, com, kept, *carried = call(
            functools.partial(next_kernel, j),
            (exchange(send), com, kept, fixed, fac, index, code, *carried),
            (((2048, 128), bf16), matrices, messages, matrices, messages),
            (elements, terms, both),
        )
    recv = exchange(send)
    (send,) = call(
        last_elements,
        (recv, kept, carried[1], fac, index, code),
        (((1024, 128), bf16),),
        (elements, terms, both, messages),
    )
    blocks = call(
        last_matrices,
        (recv, com, carried[0], fixed, send),
        (block, block, block, block),
        (both, matrices),
        any_at=(4,),
    )
    recv = to_elements(send, 8)
    base = call(base_kernel, (rho_real, rho_imag, *along_row(*blocks)), (part, part))
    return tuple(call(sum_kernel, (*base, recv), (part, part), (messages,)))


def solution(mesh):
    placed = (
        P("aux", "row", None),
        P("aux", "row", None),
        P(),
        P("aux"),
        P("aux", None, None),
        P(),
        P(),
    )
    return jax.shard_map(
        shards,
        mesh=mesh,
        in_specs=placed,
        out_specs=(P("aux", "row", None), P("aux", "row", None)),
        check_vma=False,
    )
```
